128 devices in a mesh: grp: 4 (over z), inner: 32 (over y, x, core).
Axes of the slice: x: 4, y: 4, z: 4, core: 2. Of those that a mesh axis runs over, the one named last changes fastest.
Arguments:
- averaged_features: bfloat16 [131072, 1152], P(('grp', 'inner')), may hold values from -6 to 6
- caption_embeddings_raw: bfloat16 [131072, 1152], P(('grp', 'inner')), may hold values from -6 to 6
- mapping_matrix: bfloat16 [1152, 1152], replicated, may hold values from -0.1875 to 0.1875
- logit_scaling: float32 [1], replicated, may hold values from 5 to 15
- logit_offset: float32 [1], replicated, may hold values from -3 to -1
- partner_picture_segment: int32 [4, 32, 4, 2], P(None, 'inner'), may hold values from 0 to 1
- partner_caption_segment: int32 [4, 32, 4, 2], P(None, 'inner'), may hold values from 0 to 1, as said below
- active_partner_total: int32 [4, 32, 4], P(None, 'inner'), may hold values from 0 to 2, as said below
Outputs:
- row_loss: float32 [131072], P(('grp', 'inner'))
- d_pooled: bfloat16 [131072, 1152], P(('grp', 'inner'))
- d_text: bfloat16 [131072, 1152], P(('grp', 'inner'))
- d_head: float32 [1152, 1152], P('inner')
The draws below stay inside these ranges and needn't reach their ends.
Inputs may be any that keep to these rules, and one draw needn't show every extreme that they name: `partner_caption_segment`: the 2 text blocks of one (g, i, h) are distinct. active_partner_total[g, i, g] is 0; the value 2 is taken in every draw.
All inputs are finite; a program needn't handle non-finite values.
Results may differ from the reference program's by a relative error of at most 0.023.
Values may be sent and summed in bfloat16 or wider, within the bound.
A program may use at most 192 MiB of HBM per device.

```python
import math
import jax
import jax.numpy as jnp
from jax import lax

D = 1152
BLK = 512
NBD = 2
PER_GRP = 2
GROUPS = 4
COLS = 32
BLOCKS = 256
ROWS = 131072


def draw_partner_caption_segment(key, part):
    key = jax.random.fold_in(key, 11)
    scores = jax.random.randint(key, (GROUPS, COLS, GROUPS, NBD), 0, 1 << 20) * NBD + jnp.arange(NBD, dtype=jnp.int32)
    ranked = jnp.argsort(scores, axis=-1, stable=True)
    return ranked[..., :PER_GRP].astype(jnp.int32)


def draw_active_partner_total(key, part):
    key = jax.random.fold_in(key, 23)
    counts = jax.random.randint(key, (GROUPS, COLS, GROUPS), 0, PER_GRP + 1)
    same_group = jnp.arange(GROUPS)[:, None, None] == jnp.arange(GROUPS)[None, None, :]
    counts = jnp.where(same_group, 0, counts)
    counts = counts.at[0, 0, 1].set(PER_GRP)
    return counts.astype(jnp.int32)


def touch_ends(values, stream_key, smallest, high):
    shape = values.shape
    place = [jax.random.randint(jax.random.fold_in(stream_key, axis), (), 0, shape[axis]) for axis in range(len(shape))]
    values = values.at[tuple(place)].set(smallest)
    longest = shape.index(max(shape))
    place[longest] = (place[longest] + 1) % shape[longest]
    return values.at[tuple(place)].set(high)


def steps_of(rng, shape, pieces, least, top_value):
    factor_of = 1.0
    for axis_at, parts in pieces:
        draws = jax.random.uniform(jax.random.fold_in(jax.random.fold_in(rng, 6), axis_at), (parts,), jnp.float32, least / len(pieces), top_value / len(pieces))
        factor_of = factor_of * jnp.repeat(jnp.exp(draws), shape[axis_at] // parts).reshape((-1,) + (1,) * (len(shape) - 1 - axis_at))
    return factor_of


def gaussian(own_key, extent, scale, bound, cuts=(), kind=jnp.bfloat16):
    factor_of = steps_of(own_key, extent, cuts, -0.22, 0.18) if cuts else 1.0
    entries = jax.random.normal(own_key, extent, jnp.float32) * scale * factor_of
    return jnp.minimum(jnp.maximum(entries, -bound), bound).astype(kind)


def setup_inputs(seed: int = 0) -> dict:
    key_of = jax.random.split(jax.random.key(seed), 9)
    averaged_features = gaussian(key_of[0], (ROWS, D), 1.0, 6.0, ((0, 128),))
    caption_embeddings_raw = gaussian(key_of[1], (ROWS, D), 1.0, 6.0, ((0, 128),))
    mapping_matrix = gaussian(key_of[2], (D, D), D ** -0.5, 0.1875)
    logit_scaling = jnp.clip(jnp.exp(jax.random.uniform(key_of[3], (1,), jnp.float32, math.log(5.0), math.log(15.0))), 5.0, 15.0)
    logit_offset = jnp.clip(jax.random.uniform(key_of[4], (1,), jnp.float32, -3.0, -1.0), -3.0, -1.0)
    partner_picture_segment = touch_ends(jax.random.randint(key_of[5], (GROUPS, COLS, GROUPS, PER_GRP), 0, NBD), jax.random.fold_in(key_of[5], 1), 0, NBD - 1).astype(jnp.int32)
    partner_caption_segment = draw_partner_caption_segment(jax.random.fold_in(key_of[8], 71), 0)
    active_partner_total = draw_active_partner_total(jax.random.fold_in(key_of[8], 71), 0)
    return dict(averaged_features=averaged_features, caption_embeddings_raw=caption_embeddings_raw, mapping_matrix=mapping_matrix, logit_scaling=logit_scaling, logit_offset=logit_offset, partner_picture_segment=partner_picture_segment, partner_caption_segment=partner_caption_segment, active_partner_total=active_partner_total)


NORM_EPSILON = 1e-06

def unit_rows(values):
    reciprocal_norm = lax.rsqrt(lax.optimization_barrier(jnp.sum(values * values, axis=-1, keepdims=True)) + NORM_EPSILON)
    return (values * reciprocal_norm, reciprocal_norm)

def patch_contributions(picture_segment, caption_segment, scaling_scalar, offset_scalar, matching_term, active_filter):
    similarity_scores_raw = scaling_scalar * jnp.dot(picture_segment, caption_segment.T, preferred_element_type=jnp.float32) + offset_scalar
    label_sign = 2.0 * matching_term - 1.0
    line_contributions = lax.optimization_barrier(jnp.sum(jax.nn.softplus(-label_sign * similarity_scores_raw), axis=1)) * active_filter
    derivative_patch = (-label_sign * jax.nn.sigmoid(-label_sign * similarity_scores_raw) * active_filter).astype(jnp.bfloat16)
    picture_derivative = scaling_scalar * jnp.dot(derivative_patch, caption_segment, preferred_element_type=jnp.float32)
    caption_derivative = scaling_scalar * jnp.dot(derivative_patch.T, picture_segment, preferred_element_type=jnp.float32)
    return (line_contributions, picture_derivative, caption_derivative)

def project_back(grad_unit, unit32, reciprocal_norm):
    along = lax.optimization_barrier(jnp.sum(grad_unit * unit32, axis=-1, keepdims=True))
    return (grad_unit - unit32 * along) * reciprocal_norm

def reference(averaged_features, caption_embeddings_raw, mapping_matrix, logit_scaling, logit_offset, partner_picture_segment, partner_caption_segment, active_partner_total):
    embedded = jnp.dot(averaged_features, mapping_matrix, preferred_element_type=jnp.float32)
    image_unit32, image_inv = unit_rows(embedded)
    text_unit32, text_inv = unit_rows(caption_embeddings_raw.astype(jnp.float32))
    picture_segments = image_unit32.astype(jnp.bfloat16).reshape(BLOCKS, BLK, D)
    caption_segments = text_unit32.astype(jnp.bfloat16).reshape(BLOCKS, BLK, D)
    scaling_scalar = logit_scaling[0]
    offset_scalar = logit_offset[0]
    identity_matrix = jnp.eye(BLK, dtype=jnp.float32)
    mismatched_term = jnp.zeros((BLK, BLK), jnp.float32)

    def diagonal_tile(matched_partners):
        return patch_contributions(matched_partners[0], matched_partners[1], scaling_scalar, offset_scalar, identity_matrix, 1.0)
    row_sums, image_grads, text_grads = lax.map(diagonal_tile, (picture_segments, caption_segments))
    image_group = jnp.arange(GROUPS, dtype=jnp.int32)[:, None, None, None]
    column = jnp.arange(COLS, dtype=jnp.int32)[None, :, None, None]
    text_group = jnp.arange(GROUPS, dtype=jnp.int32)[None, None, :, None]
    slot_index = jnp.arange(PER_GRP, dtype=jnp.int32)[None, None, None, :]
    image_index = ((image_group * COLS + column) * NBD + partner_picture_segment).reshape(-1).astype(jnp.int32)
    text_index = ((text_group * COLS + column) * NBD + partner_caption_segment).reshape(-1).astype(jnp.int32)
    live_list = (slot_index < active_partner_total[..., None]).astype(jnp.float32).reshape(-1)

    def hard_step(carry, entry):
        row_accumulator, image_acc, text_acc = carry
        picture_position, caption_position, active_filter = entry
        line_contributions, picture_derivative, caption_derivative = patch_contributions(picture_segments[picture_position], caption_segments[caption_position], scaling_scalar, offset_scalar, mismatched_term, active_filter)
        rounded = lax.optimization_barrier(caption_derivative.astype(jnp.bfloat16)).astype(jnp.float32)
        return ((row_accumulator.at[picture_position].add(line_contributions), image_acc.at[picture_position].add(picture_derivative), text_acc.at[caption_position].add(rounded)), None)
    (row_sums, image_grads, text_grads), unused = lax.scan(hard_step, (row_sums, image_grads, text_grads), (image_index, text_index, live_list))
    embed_grad = project_back(image_grads.reshape(ROWS, D), image_unit32, image_inv).astype(jnp.bfloat16)
    d_pooled = jnp.dot(embed_grad, mapping_matrix.T, preferred_element_type=jnp.float32).astype(jnp.bfloat16)
    d_text = project_back(text_grads.reshape(ROWS, D), text_unit32, text_inv).astype(jnp.bfloat16)
    d_head = jnp.dot(averaged_features.T, embed_grad, preferred_element_type=jnp.float32)
    row_loss = row_sums.reshape(ROWS) / BLK
    return (row_loss, d_pooled, d_text, d_head)
```

```python
import functools

import jax
import jax.numpy as jnp
from jax import lax
from jax.experimental import pallas as pl
from jax.experimental.pallas import tpu as pltpu
from jax.sharding import PartitionSpec as P

MESH = pl.DeviceIdType.MESH
BLK = 512
D = 1152
ROWS = 1024
CH = 256
NCH = ROWS // CH
EPS = 1e-06
HR = 36
HP = 48
LO = 512
HI = D - LO
BF = jnp.bfloat16
F32 = jnp.float32

NN = (((1,), (0,)), ((), ()))
NT = (((1,), (1,)), ((), ()))
TN = (((0,), (0,)), ((), ()))


def mm(a, b, dims):
    return lax.dot_general(a, b, dims, preferred_element_type=F32)


def kernel(
    f_hbm, t_hbm, w_hbm, scale_ref, offset_ref, img_ref, cap_ref, cnt_ref,
    loss_out, pooled_out, text_out, head_out,
    fn, fp, tn, tun, tq, w, iun, iup, unit32, din, wide, si, st, ri, rt, gs, ep,
    hs, rc, rx, ry, ba, bb, r2a, r2b, zs, zr, inv_i, inv_t, loss_n, loss_p, ls, lr,
    f_send, f_recv, t_send, t_recv, di_send, di_recv, dt_send, dt_recv,
    l_sem, c_sem, x_send, x_recv, y_send, y_recv, x2_send, x2_recv, y2_send, y2_recv,
    z_send, z_recv, in_sem, out_sem,
):
    me = lax.axis_index("grp")
    inner = lax.axis_index("inner")
    odd = lax.rem(me, 2)
    gp = lax.rem(me + 3 + 2 * odd, 4)
    gq = lax.rem(me + 1 + 2 * odd, 4)
    core = lax.rem(inner, 2)
    x = lax.rem(inner // 2, 4)
    y = inner // 8

    def at(yy, xx, cc):
        return (yy * 4 + xx) * 2 + cc

    p_dev, q_dev = (gp, inner), (gq, inner)
    c_dev = (me, at(y, x, 1 - core))
    xs = [lax.rem(x + d, 4) for d in (1, 2, 3)]
    ys = [lax.rem(y + d, 4) for d in (1, 2, 3)]
    x_devs = [(me, at(y, v, core)) for v in xs]
    y_devs = [(me, at(v, x, core)) for v in ys]

    def remote(src, dst, send, recv, dev):
        return pltpu.make_async_remote_copy(
            src_ref=src, dst_ref=dst, send_sem=send, recv_sem=recv, device_id=dev, device_id_type=MESH
        )

    barrier = pltpu.get_barrier_semaphore()
    peers = [p_dev, q_dev, c_dev] + x_devs + y_devs
    for dev in peers:
        pl.semaphore_signal(barrier, inc=1, device_id=dev, device_id_type=MESH)
    pl.semaphore_wait(barrier, len(peers))

    def rows(c):
        return pl.ds(pl.multiple_of(c * CH, CH), CH)

    def half(c):
        return pl.ds(pl.multiple_of(lax.rem(c, 2) * CH, CH), CH)

    def f_copy(c):
        return remote(f_hbm.at[rows(c)], fp.at[rows(c)], f_send.at[c], f_recv.at[c], p_dev)

    def t_copy(c):
        return remote(t_hbm.at[rows(c)], tq.at[c // 2, half(c)], t_send.at[c], t_recv.at[c], q_dev)

    def di_copy(c):
        return remote(si.at[rows(c)], ri.at[rows(c)], di_send.at[c], di_recv.at[c], p_dev)

    def dt_copy(c):
        return remote(st.at[rows(c)], rt.at[rows(c)], dt_send.at[c], dt_recv.at[c], q_dev)

    for c in range(NCH):
        f_copy(c).start()
        t_copy(c).start()
    w_in = pltpu.make_async_copy(w_hbm, w, in_sem.at[0])
    f_in = pltpu.make_async_copy(f_hbm, fn, in_sem.at[1])
    t_in = pltpu.make_async_copy(t_hbm, tn, in_sem.at[2])
    w_in.start()
    f_in.start()
    t_in.start()

    scale = scale_ref[0]
    offset = offset_ref[0]

    def pair(g, h):
        first = cap_ref[g, 0, h, 0]
        a0, a1, live = img_ref[g, 0, h, 0], img_ref[g, 0, h, 1], cnt_ref[g, 0, h]
        out = []
        for k in range(2):
            slot = jnp.abs(first - k)
            out.append((a0 + (a1 - a0) * slot, jnp.clip(live - slot, 0, 1).astype(F32)))
        return out

    pair_a, pair_b, pair_c = pair(gp, me), pair(me, gq), pair(gp, gq)

    def hit(sel, b):
        return (1 - jnp.abs(sel - b)).astype(F32)

    def norm(v):
        return lax.rsqrt(jnp.sum(v * v, axis=-1, keepdims=True) + EPS)

    def project(g, u, inv):
        return (g - u * jnp.sum(g * u, axis=-1, keepdims=True)) * inv

    def loop(n, body, start=0):
        lax.fori_loop(start, n, lambda i, _: (body(i), 0)[1], 0)

    def embed(f_ref, c):
        e = mm(f_ref[rows(c), :], w[...], NN)
        inv = norm(e)
        return e * inv, inv

    w_in.wait()
    f_in.wait()

    def embed_own(c):
        unit, inv = embed(fn, c)
        unit32[rows(c), :] = unit
        inv_i[rows(c), :] = inv
        iun[c // 2, half(c), :] = unit.astype(BF)

    loop(NCH, embed_own)
    t_in.wait()

    def text_own(c):
        v = tn[rows(c), :].astype(F32)
        inv = norm(v)
        inv_t[rows(c), :] = inv
        tun[c // 2, half(c), :] = (v * inv).astype(BF)

    loop(NCH, text_own)

    def tile(images, sel, texts, k, slot, live, diagonal):
        def body(r):
            s = mm(images[sel, half(r), :], texts[k], NT) * scale + offset
            if diagonal:
                on = (lax.broadcasted_iota(jnp.int32, s.shape, 0) + r * CH) == lax.broadcasted_iota(jnp.int32, s.shape, 1)
                s = jnp.where(on, -s, s)
            e = jnp.exp(s)
            g = e / (1.0 + e)
            if diagonal:
                g = jnp.where(on, -g, g)
            else:
                g = g * live
            gs[slot, half(r), :] = g.astype(BF)
            total = jnp.sum(jnp.log1p(e), axis=1, keepdims=True)
            return total

        return body

    def tile_diag(k):
        body = tile(iun, k, tun, k, k, None, True)

        def step(r):
            loss_n[k, half(r), :] = body(r)

        loop(2, step)

    def tile_hard(images, texts, pr, k, slot, acc, first=False):
        sel, live = pr[k]
        body = tile(images, sel, texts, k, slot, live, False)

        def step(r):
            total = body(r) * live
            for b in range(2):
                v = total * hit(sel, b)
                if first:
                    acc[b, half(r), :] = v
                else:
                    acc[b, half(r), :] = acc[b, half(r), :] + v

        loop(2, step)

    loop(2, tile_diag)

    def arrive(c):
        f_copy(c).wait_recv()
        unit, _ = embed(fp, c)
        iup[c // 2, half(c), :] = unit.astype(BF)
        t_copy(c).wait_recv()
        v = tq[c // 2, half(c), :].astype(F32)
        tq[c // 2, half(c), :] = (v * norm(v)).astype(BF)

    loop(2, arrive)
    tile_hard(iun, tq, pair_b, 0, 4, loss_n)
    loop(4, arrive, 2)

    def back_text(c, parts):
        cols = half(c)
        out = None
        for slot, images, sel in parts:
            v = mm(gs[slot, :, cols], images[sel], TN)
            out = v if out is None else out + v
        return out * scale

    def back_image(c, parts):
        b = c // 2
        out = None
        for slot, texts, k, sel in parts:
            g = gs[slot, half(c), :]
            if sel is not None:
                g = (g.astype(F32) * hit(sel, b)).astype(BF)
            v = mm(g, texts[k], NN)
            out = v if out is None else out + v
        return out * scale

    def send_text(k):
        def step(c):
            st[rows(c), :] = back_text(c, ((4 + k, iun, pair_b[k][0]), (6 + k, iup, pair_c[k][0]))).astype(BF)
            dt_copy(c).start()

        loop(2 * k + 2, step, 2 * k)

    tile_hard(iup, tq, pair_c, 0, 6, loss_p, True)
    send_text(0)
    tile_hard(iup, tun, pair_a, 0, 2, loss_p)
    tile_hard(iup, tun, pair_a, 1, 3, loss_p)
    tile_hard(iup, tq, pair_c, 1, 7, loss_p)

    def send_image(c):
        g = back_image(
            c,
            ((2, tun, 0, pair_a[0][0]), (3, tun, 1, pair_a[1][0]), (6, tq, 0, pair_c[0][0]), (7, tq, 1, pair_c[1][0])),
        )
        si[rows(c), :] = g.astype(BF)
        di_copy(c).start()
        unit, inv = embed(fp, c)
        ep[rows(c), :] = project(g, unit, inv).astype(BF)

    loop(NCH, send_image)

    def row_form(ref, out):
        for i in range(8):
            v = ref[i // 4, pl.ds((i % 4) * 128, 128), :]
            out[pl.ds(i, 1), :] = jnp.transpose(jnp.broadcast_to(v, (128, 128)))[0:1, :]

    row_form(loss_p, ls)
    l_copy = remote(ls, lr, l_sem.at[0], l_sem.at[1], p_dev)
    l_copy.start()
    tile_hard(iun, tq, pair_b, 1, 5, loss_n)
    send_text(1)

    def own_image(c):
        b = c // 2
        g = mm(gs[b, half(c), :], tun[b], NN) * scale
        g = g + back_image(c, ((4, tq, 0, pair_b[0][0]), (5, tq, 1, pair_b[1][0])))
        din[rows(c), :] = g

    loop(NCH, own_image)

    def own_embed_grad(c):
        tq[c // 2, half(c), :] = project(din[rows(c), :], unit32[rows(c), :], inv_i[rows(c), :]).astype(BF)

    loop(NCH, own_embed_grad)

    def head(j):
        cols = pl.ds(pl.multiple_of(j * 384, 128), 384)
        h = mm(fp[:, cols], ep[...], TN)
        h = h + mm(fn[pl.ds(0, BLK), cols], tq[0], TN) + mm(fn[pl.ds(BLK, BLK), cols], tq[1], TN)
        wide[pl.ds(pl.multiple_of(j * 384, 128), 384), :] = h

    loop(3, head)

    zero = jnp.zeros((HP - HR, D), F32)

    def split(j):
        v = wide[pl.ds(pl.multiple_of(j * 2 * HR, 8), 2 * HR), :]
        for c in range(2):
            hs[j, c] = jnp.concatenate([v[c * HR : (c + 1) * HR, :], zero], axis=0).astype(BF)

    loop(16, split)
    c_copy = remote(hs.at[:, 1 - core], rc, c_sem.at[0], c_sem.at[1], c_dev)
    c_copy.start()

    def own_text(c):
        b = c // 2
        sel = jnp.where(b == 0, pair_a[0][0], pair_a[1][0])
        v = mm(gs[b, :, half(c)], iun[b], TN) + mm(gs[2 + b, :, half(c)], iup[sel], TN)
        wide[rows(c), :] = v * scale

    loop(NCH, own_text)

    c_copy.wait()

    def add_core(j):
        rc[j] = (rc[j].astype(F32) + hs[j, core].astype(F32)).astype(BF)

    loop(16, add_core)

    xc = []
    yc = []
    for d in range(3):
        xc += [
            remote(
                rc.at[pl.ds(yy * 4 + xs[d], 1), :, pl.ds(0, LO)], rx.at[d, pl.ds(yy, 1)],
                x_send.at[d, yy], x_recv.at[d, yy], x_devs[d],
            )
            for yy in range(4)
        ]
        yc.append(
            remote(
                rc.at[pl.ds(ys[d] * 4, 4), :, pl.ds(LO, HI)], ry.at[d],
                y_send.at[d], y_recv.at[d], y_devs[d],
            )
        )
    for copy in xc + yc:
        copy.start()

    def finish(c):
        di_copy(c).wait_recv()
        g = din[rows(c), :] + ri[rows(c), :].astype(F32)
        eg = project(g, unit32[rows(c), :], inv_i[rows(c), :]).astype(BF)
        iup[c // 2, half(c), :] = mm(eg, w[...], NT).astype(BF)
        pltpu.make_async_copy(iup.at[c // 2, half(c)], pooled_out.at[rows(c)], out_sem.at[0, c]).start()
        dt_copy(c).wait_recv()
        inv = inv_t[rows(c), :]
        u = tn[rows(c), :].astype(F32) * inv
        gt = wide[rows(c), :] + rt[rows(c), :].astype(F32)
        iun[c // 2, half(c), :] = project(gt, u, inv).astype(BF)
        pltpu.make_async_copy(iun.at[c // 2, half(c)], text_out.at[rows(c)], out_sem.at[1, c]).start()

    loop(2, finish)

    for copy in xc + yc:
        copy.wait()

    def add_x(yy):
        v = rc[yy * 4 + x, :, pl.ds(0, LO)].astype(F32)
        for d in range(3):
            v = v + rx[d, yy].astype(F32)
        ba[yy] = v.astype(BF)

    def add_y(xx):
        v = rc[y * 4 + xx, :, pl.ds(LO, HI)].astype(F32)
        for d in range(3):
            v = v + ry[d, xx].astype(F32)
        bb[xx] = v.astype(BF)

    loop(4, add_x)
    loop(4, add_y)
    second = []
    for d in range(3):
        second.append(remote(ba.at[ys[d]], r2a.at[d], y2_send.at[d], y2_recv.at[d], y_devs[d]))
        second.append(remote(bb.at[xs[d]], r2b.at[d], x2_send.at[d], x2_recv.at[d], x_devs[d]))
    for copy in second:
        copy.start()
    loop(3, finish, 2)
    for copy in second:
        copy.wait()
    lo = ba[y].astype(F32)
    hi = bb[x].astype(F32)
    for d in range(3):
        lo = lo + r2a[d].astype(F32)
        hi = hi + r2b[d].astype(F32)
    zs[0, :, pl.ds(0, LO)] = lo.astype(BF)
    zs[0, :, pl.ds(LO, HI)] = hi.astype(BF)
    z0 = remote(zs.at[0], zr.at[0], z_send.at[0], z_recv.at[0], p_dev)
    z0.start()
    z0.wait()
    zs[1] = (zs[0].astype(F32) + zr[0].astype(F32)).astype(BF)
    z1 = remote(zs.at[1], zr.at[1], z_send.at[1], z_recv.at[1], q_dev)
    z1.start()
    loop(4, finish, 3)
    l_copy.wait()
    row_form(loss_n, ls)
    loss_out[...] = (ls[...] + lr[...]) * (1.0 / BLK)
    z1.wait()
    head_out[...] = (zs[1].astype(F32) + zr[1].astype(F32))[0:HR, :]

    def drain(c):
        f_copy(c).wait_send()
        t_copy(c).wait_send()
        di_copy(c).wait_send()
        dt_copy(c).wait_send()
        pltpu.make_async_copy(iup.at[c // 2, half(c)], pooled_out.at[rows(c)], out_sem.at[0, c]).wait()
        pltpu.make_async_copy(iun.at[c // 2, half(c)], text_out.at[rows(c)], out_sem.at[1, c]).wait()

    loop(NCH, drain)


def per_device(features, captions, head, scaling, offset, img, cap, cnt):
    hbm = pl.BlockSpec(memory_space=pl.ANY)
    smem = pl.BlockSpec(memory_space=pltpu.SMEM)
    vmem = pl.BlockSpec(memory_space=pltpu.VMEM)
    big = pltpu.VMEM((ROWS, D), BF)
    blocks = pltpu.VMEM((2, BLK, D), BF)
    column = pltpu.VMEM((ROWS, 1), F32)
    dma = pltpu.SemaphoreType.DMA
    loss, pooled, text, grad = pl.pallas_call(
        kernel,
        out_shape=(
            jax.ShapeDtypeStruct((8, 128), F32),
            jax.ShapeDtypeStruct((ROWS, D), BF),
            jax.ShapeDtypeStruct((ROWS, D), BF),
            jax.ShapeDtypeStruct((HR, D), F32),
        ),
        in_specs=[hbm] * 3 + [smem] * 5,
        out_specs=(vmem, hbm, hbm, vmem),
        scratch_shapes=[
            big, big, big, blocks, blocks, pltpu.VMEM((D, D), BF), blocks, blocks,
            pltpu.VMEM((ROWS, D), F32), pltpu.VMEM((ROWS, D), F32), pltpu.VMEM((D, D), F32),
            big, big, big, big, pltpu.VMEM((8, BLK, BLK), BF), big,
            pltpu.VMEM((16, 2, HP, D), BF), pltpu.VMEM((16, HP, D), BF),
            pltpu.VMEM((3, 4, HP, LO), BF), pltpu.VMEM((3, 4, HP, HI), BF),
            pltpu.VMEM((4, HP, LO), BF), pltpu.VMEM((4, HP, HI), BF),
            pltpu.VMEM((3, HP, LO), BF), pltpu.VMEM((3, HP, HI), BF),
            pltpu.VMEM((2, HP, D), BF), pltpu.VMEM((2, HP, D), BF),
            column, column, pltpu.VMEM((2, BLK, 1), F32), pltpu.VMEM((2, BLK, 1), F32),
            pltpu.VMEM((8, 128), F32), pltpu.VMEM((8, 128), F32),
            dma((NCH,)), dma((NCH,)), dma((NCH,)), dma((NCH,)), dma((NCH,)), dma((NCH,)), dma((NCH,)), dma((NCH,)),
            dma((2,)), dma((2,)), dma((3, 4)), dma((3, 4)), dma((3,)), dma((3,)), dma((3,)), dma((3,)), dma((3,)), dma((3,)),
            dma((2,)), dma((2,)), dma((3,)), dma((2, NCH)),
        ],
        compiler_params=pltpu.CompilerParams(
            collective_id=0, has_side_effects=True, vmem_limit_bytes=63 << 20
        ),
        cost_estimate=pl.CostEstimate(flops=34_000_000_000, bytes_accessed=20_000_000, transcendentals=6_000_000),
    )(features, captions, head, scaling, offset, img, cap, cnt)
    return loss.reshape(ROWS), pooled, text, grad


def solution(mesh):
    return jax.shard_map(
        per_device,
        mesh=mesh,
        in_specs=(
            P(("grp", "inner"), None),
            P(("grp", "inner"), None),
            P(),
            P(),
            P(),
            P(None, "inner", None, None),
            P(None, "inner", None, None),
            P(None, "inner", None),
        ),
        out_specs=(
            P(("grp", "inner")),
            P(("grp", "inner"), None),
            P(("grp", "inner"), None),
            P("inner", None),
        ),
        check_vma=False,
    )
```

```python
import functools

import jax
import jax.numpy as jnp
from jax import lax
from jax.experimental import pallas as pl
from jax.experimental.pallas import tpu as pltpu
from jax.sharding import PartitionSpec as P

MESH = pl.DeviceIdType.MESH
BLK = 512
D = 1152
ROWS = 1024
CH = 256
NCH = ROWS // CH
SM = 128
NSM = ROWS // SM
EPS = 1e-06
HR = 36
HP = 48
LO = 512
HI = D - LO
BF = jnp.bfloat16
F32 = jnp.float32

NN = (((1,), (0,)), ((), ()))
NT = (((1,), (1,)), ((), ()))
TN = (((0,), (0,)), ((), ()))


def mm(a, b, dims):
    return lax.dot_general(a, b, dims, preferred_element_type=F32)


def kernel(
    f_hbm, t_hbm, w_hbm, scale_ref, offset_ref, img_ref, cap_ref, cnt_ref,
    loss_out, pooled_out, text_out, head_out,
    fn, fp, tn, tun, tq, w, iun, iup, unit32, din, wide, si, st, ri, rt, gs, ep,
    hs_lo, hs_hi, rc_lo, rc_hi, rx, ry, ba, bb, r2a, r2b, zs, zr, inv, loss_n, loss_p, ls, lr,
    f_send, f_recv, t_send, t_recv, di_send, di_recv, dt_send, dt_recv,
    l_sem, c_sem, x_send, x_recv, y_send, y_recv, x2_send, x2_recv, y2_send, y2_recv,
    z_send, z_recv, in_sem, out_sem,
):
    me = lax.axis_index("grp")
    inner = lax.axis_index("inner")
    odd = lax.rem(me, 2)
    gp = lax.rem(me + 3 + 2 * odd, 4)
    gq = lax.rem(me + 1 + 2 * odd, 4)
    core = lax.rem(inner, 2)
    x = lax.rem(inner // 2, 4)
    y = inner // 8

    def at(yy, xx, cc):
        return (yy * 4 + xx) * 2 + cc

    p_dev, q_dev = (gp, inner), (gq, inner)
    c_dev = (me, at(y, x, 1 - core))
    xs = [lax.rem(x + d, 4) for d in (1, 2, 3)]
    ys = [lax.rem(y + d, 4) for d in (1, 2, 3)]
    x_devs = [(me, at(y, v, core)) for v in xs]
    y_devs = [(me, at(v, x, core)) for v in ys]

    def remote(src, dst, send, recv, dev):
        return pltpu.make_async_remote_copy(
            src_ref=src, dst_ref=dst, send_sem=send, recv_sem=recv, device_id=dev, device_id_type=MESH
        )

    barrier = pltpu.get_barrier_semaphore()
    peers = [p_dev, q_dev, c_dev] + x_devs + y_devs
    for dev in peers:
        pl.semaphore_signal(barrier, inc=1, device_id=dev, device_id_type=MESH)
    pl.semaphore_wait(barrier, len(peers))

    def rows(c):
        return pl.ds(pl.multiple_of(c * CH, CH), CH)

    def half(c):
        return pl.ds(pl.multiple_of(lax.rem(c, 2) * CH, CH), CH)

    def small(c):
        return pl.ds(pl.multiple_of(c * SM, SM), SM)

    def part(c):
        return pl.ds(pl.multiple_of(lax.rem(c, 4) * SM, SM), SM)

    def f_copy(c):
        return remote(f_hbm.at[small(c)], fp.at[small(c)], f_send.at[c], f_recv.at[c], p_dev)

    def t_copy(c):
        return remote(t_hbm.at[small(c)], tq.at[c // 4, part(c)], t_send.at[c], t_recv.at[c], q_dev)

    def di_copy(c):
        return remote(si.at[rows(c)], ri.at[rows(c)], di_send.at[c], di_recv.at[c], p_dev)

    def dt_copy(c):
        return remote(st.at[rows(c)], rt.at[rows(c)], dt_send.at[c], dt_recv.at[c], q_dev)

    for c in range(NSM):
        f_copy(c).start()
        t_copy(c).start()
    w_in = pltpu.make_async_copy(w_hbm, w, in_sem.at[0])
    f_in = pltpu.make_async_copy(f_hbm, fn, in_sem.at[1])
    t_in = pltpu.make_async_copy(t_hbm, tn, in_sem.at[2])
    w_in.start()
    f_in.start()
    t_in.start()

    scale = scale_ref[0]
    offset = offset_ref[0]

    def pair(g, h):
        first = cap_ref[g, 0, 0, h]
        a0, a1, live = img_ref[g, 0, 0, h], img_ref[g, 0, 1, h], cnt_ref[g, 0, h]
        out = []
        for k in range(2):
            slot = jnp.abs(first - k)
            out.append((a0 + (a1 - a0) * slot, jnp.clip(live - slot, 0, 1).astype(F32)))
        return out

    pair_a, pair_b, pair_c = pair(gp, me), pair(me, gq), pair(gp, gq)

    def hit(sel, b):
        return (1 - jnp.abs(sel - b)).astype(F32)

    def norm(v):
        return lax.rsqrt(jnp.sum(v * v, axis=-1, keepdims=True) + EPS)

    def project(g, u, r):
        return (g - u * jnp.sum(g * u, axis=-1, keepdims=True)) * r

    def loop(n, body, start=0):
        lax.fori_loop(start, n, lambda i, _: (body(i), 0)[1], 0)

    def embed(f_ref, where):
        e = mm(f_ref[where, :], w[...], NN)
        r = norm(e)
        return e * r, r

    w_in.wait()
    f_in.wait()

    def embed_own(c):
        unit, r = embed(fn, rows(c))
        unit32[rows(c), :] = unit
        inv[rows(c), 0:1] = r
        iun[c // 2, half(c), :] = unit.astype(BF)

    loop(NCH, embed_own)
    t_in.wait()

    def text_own(c):
        v = tn[rows(c), :].astype(F32)
        r = norm(v)
        inv[rows(c), 2:3] = r
        tun[c // 2, half(c), :] = (v * r).astype(BF)

    loop(NCH, text_own)

    def tile(images, sel, texts, k, slot, live, diagonal):
        def body(r):
            s = mm(images[sel, half(r), :], texts[k], NT) * scale + offset
            if diagonal:
                on = (lax.broadcasted_iota(jnp.int32, s.shape, 0) + r * CH) == lax.broadcasted_iota(jnp.int32, s.shape, 1)
                s = jnp.where(on, -s, s)
            e = jnp.exp(s)
            g = e / (1.0 + e)
            if diagonal:
                g = jnp.where(on, -g, g)
            else:
                g = g * live
            gs[slot, half(r), :] = g.astype(BF)
            total = jnp.sum(jnp.log1p(e), axis=1, keepdims=True)
            return total

        return body

    def tile_diag(k):
        body = tile(iun, k, tun, k, k, None, True)

        def step(r):
            loss_n[k, half(r), :] = body(r)

        loop(2, step)

    def tile_hard(images, texts, pr, k, slot, acc, first=False):
        sel, live = pr[k]
        body = tile(images, sel, texts, k, slot, live, False)

        def step(r):
            total = body(r) * live
            for b in range(2):
                v = total * hit(sel, b)
                if first:
                    acc[b, half(r), :] = v
                else:
                    acc[b, half(r), :] = acc[b, half(r), :] + v

        loop(2, step)

    loop(2, tile_diag)

    def own_diag(c):
        b = c // 2
        din[rows(c), :] = mm(gs[b, half(c), :], tun[b], NN) * scale

    loop(NCH, own_diag)

    def arrive(c):
        b = c // 4
        f_copy(c).wait_recv()
        unit, r = embed(fp, small(c))
        wide[small(c), :] = unit
        inv[small(c), 1:2] = r
        u = unit.astype(BF)
        iup[b, part(c), :] = u
        total = None
        for k in range(2):
            sel, live = pair_a[k]
            keep = live * hit(sel, b)
            e = jnp.exp(mm(u, tun[k], NT) * scale + offset)
            gs[2 + 2 * k + b, part(c), :] = (e / (1.0 + e) * keep).astype(BF)
            v = jnp.sum(jnp.log1p(e), axis=1, keepdims=True) * keep
            total = v if total is None else total + v
        loss_p[b, part(c), :] = total
        t_copy(c).wait_recv()
        v = tq[b, part(c), :].astype(F32)
        tq[b, part(c), :] = (v * norm(v)).astype(BF)

    loop(4, arrive)
    tile_hard(iun, tq, pair_b, 0, 6, loss_n)

    def back_text(c, parts):
        cols = half(c)
        out = None
        for slot, images, sel in parts:
            v = mm(gs[slot, :, cols], images[sel], TN)
            out = v if out is None else out + v
        return out * scale

    def back_image(c, parts):
        b = c // 2
        out = None
        for slot, texts, k, sel in parts:
            g = gs[slot, half(c), :]
            if sel is not None:
                g = (g.astype(F32) * hit(sel, b)).astype(BF)
            v = mm(g, texts[k], NN)
            out = v if out is None else out + v
        return out * scale

    def own_first(c):
        din[rows(c), :] = din[rows(c), :] + back_image(c, ((6, tq, 0, pair_b[0][0]),))

    loop(NCH, own_first)
    loop(NSM, arrive, 4)

    def send_text(c):
        k = c // 2
        sel_b = jnp.where(k == 0, pair_b[0][0], pair_b[1][0])
        sel_c = jnp.where(k == 0, pair_c[0][0], pair_c[1][0])
        st[rows(c), :] = back_text(c, ((6 + k, iun, sel_b), (8 + k, iup, sel_c))).astype(BF)
        dt_copy(c).start()

    def send_image(c):
        b = c // 2
        g = back_image(
            c,
            ((2 + b, tun, 0, None), (4 + b, tun, 1, None), (8, tq, 0, pair_c[0][0]), (9, tq, 1, pair_c[1][0])),
        )
        si[rows(c), :] = g.astype(BF)
        di_copy(c).start()
        ep[rows(c), :] = project(g, wide[rows(c), :], inv[rows(c), 1:2]).astype(BF)

    tile_hard(iup, tq, pair_c, 0, 8, loss_p)
    loop(1, send_text)
    tile_hard(iup, tq, pair_c, 1, 9, loss_p)
    loop(1, send_image)
    loop(2, send_text, 1)
    loop(NCH, send_image, 1)

    def row_form(ref, out):
        for i in range(8):
            v = ref[i // 4, pl.ds((i % 4) * 128, 128), :]
            out[pl.ds(i, 1), :] = jnp.transpose(jnp.broadcast_to(v, (128, 128)))[0:1, :]

    row_form(loss_p, ls)
    l_copy = remote(ls, lr, l_sem.at[0], l_sem.at[1], p_dev)
    l_copy.start()
    tile_hard(iun, tq, pair_b, 1, 7, loss_n)

    def own_image(c):
        g = din[rows(c), :] + back_image(c, ((7, tq, 1, pair_b[1][0]),))
        din[rows(c), :] = g
        tun[c // 2, half(c), :] = project(g, unit32[rows(c), :], inv[rows(c), 0:1]).astype(BF)

    loop(NCH, own_image)

    def head(cols, hs):
        width = cols.size

        def step(j):
            own = pl.ds(pl.multiple_of(j * 384, 128), 384)
            h = mm(fp[:, own], ep[:, cols], TN)
            h = h + mm(fn[pl.ds(0, BLK), own], tun[0, :, cols], TN) + mm(fn[pl.ds(BLK, BLK), own], tun[1, :, cols], TN)
            wide[own, cols] = h

        loop(3, step)
        zero = jnp.zeros((HP - HR, width), F32)

        def split(j):
            v = wide[pl.ds(pl.multiple_of(j * 2 * HR, 8), 2 * HR), cols]
            for c in range(2):
                hs[j, c] = jnp.concatenate([v[c * HR : (c + 1) * HR, :], zero], axis=0).astype(BF)

        loop(16, split)

    lo_cols, hi_cols = pl.ds(0, LO), pl.ds(LO, HI)
    head(lo_cols, hs_lo)
    c_lo = remote(hs_lo.at[:, 1 - core], rc_lo, c_sem.at[0], c_sem.at[1], c_dev)
    c_lo.start()
    head(hi_cols, hs_hi)
    c_hi = remote(hs_hi.at[:, 1 - core], rc_hi, c_sem.at[2], c_sem.at[3], c_dev)
    c_hi.start()
    loop(NCH, send_text, 2)

    def add_core(rc, hs):
        def step(j):
            rc[j] = (rc[j].astype(F32) + hs[j, core].astype(F32)).astype(BF)

        loop(16, step)

    c_lo.wait()
    add_core(rc_lo, hs_lo)
    xc = []
    for d in range(3):
        xc += [
            remote(
                rc_lo.at[yy * 4 + xs[d]], rx.at[d, yy], x_send.at[d, yy], x_recv.at[d, yy], x_devs[d]
            )
            for yy in range(4)
        ]
    for copy in xc:
        copy.start()
    c_hi.wait()
    add_core(rc_hi, hs_hi)
    yc = [
        remote(rc_hi.at[pl.ds(ys[d] * 4, 4)], ry.at[d], y_send.at[d], y_recv.at[d], y_devs[d]) for d in range(3)
    ]
    for copy in yc:
        copy.start()

    def own_text(c):
        b = c // 2
        sel = jnp.where(b == 0, pair_a[0][0], pair_a[1][0])
        v = mm(gs[b, :, half(c)], iun[b], TN) + mm(gs[2 + 2 * b + sel, :, half(c)], iup[sel], TN)
        wide[rows(c), :] = v * scale

    loop(NCH, own_text)

    def finish(c):
        di_copy(c).wait_recv()
        g = din[rows(c), :] + ri[rows(c), :].astype(F32)
        eg = project(g, unit32[rows(c), :], inv[rows(c), 0:1]).astype(BF)
        iup[c // 2, half(c), :] = mm(eg, w[...], NT).astype(BF)
        pltpu.make_async_copy(iup.at[c // 2, half(c)], pooled_out.at[rows(c)], out_sem.at[0, c]).start()
        dt_copy(c).wait_recv()
        r = inv[rows(c), 2:3]
        u = tn[rows(c), :].astype(F32) * r
        gt = wide[rows(c), :] + rt[rows(c), :].astype(F32)
        iun[c // 2, half(c), :] = project(gt, u, r).astype(BF)
        pltpu.make_async_copy(iun.at[c // 2, half(c)], text_out.at[rows(c)], out_sem.at[1, c]).start()

    loop(2, finish)

    def add_x(yy):
        v = rc_lo[yy * 4 + x].astype(F32)
        for d in range(3):
            v = v + rx[d, yy].astype(F32)
        ba[yy] = v.astype(BF)

    def add_y(xx):
        v = rc_hi[y * 4 + xx].astype(F32)
        for d in range(3):
            v = v + ry[d, xx].astype(F32)
        bb[xx] = v.astype(BF)

    for copy in xc:
        copy.wait()
    loop(4, add_x)
    second = [remote(ba.at[ys[d]], r2a.at[d], y2_send.at[d], y2_recv.at[d], y_devs[d]) for d in range(3)]
    for copy in second:
        copy.start()
    for copy in yc:
        copy.wait()
    loop(4, add_y)
    third = [remote(bb.at[xs[d]], r2b.at[d], x2_send.at[d], x2_recv.at[d], x_devs[d]) for d in range(3)]
    for copy in third:
        copy.start()
    loop(3, finish, 2)
    for copy in second + third:
        copy.wait()
    lo = ba[y].astype(F32)
    hi = bb[x].astype(F32)
    for d in range(3):
        lo = lo + r2a[d].astype(F32)
        hi = hi + r2b[d].astype(F32)
    zs[0, :, pl.ds(0, LO)] = lo.astype(BF)
    zs[0, :, pl.ds(LO, HI)] = hi.astype(BF)
    z0 = remote(zs.at[0], zr.at[0], z_send.at[0], z_recv.at[0], p_dev)
    z0.start()
    z0.wait()
    zs[1] = (zs[0].astype(F32) + zr[0].astype(F32)).astype(BF)
    z1 = remote(zs.at[1], zr.at[1], z_send.at[1], z_recv.at[1], q_dev)
    z1.start()
    loop(4, finish, 3)
    l_copy.wait()
    row_form(loss_n, ls)
    loss_out[...] = (ls[...] + lr[...]) * (1.0 / BLK)
    z1.wait()
    head_out[...] = (zs[1].astype(F32) + zr[1].astype(F32))[0:HR, :]

    def sent(c):
        f_copy(c).wait_send()
        t_copy(c).wait_send()

    loop(NSM, sent)

    def drain(c):
        di_copy(c).wait_send()
        dt_copy(c).wait_send()
        pltpu.make_async_copy(iup.at[c // 2, half(c)], pooled_out.at[rows(c)], out_sem.at[0, c]).wait()
        pltpu.make_async_copy(iun.at[c // 2, half(c)], text_out.at[rows(c)], out_sem.at[1, c]).wait()

    loop(NCH, drain)


def emit(loss, pooled, text, grad, loss_out, pooled_out, text_out, grad_out, stage, small, sem_in, sem_out):
    reads, writes = [], []
    for c in range(NCH):
        for i, (src, dst) in enumerate(((pooled, pooled_out), (text, text_out))):
            where = pl.ds(c * CH, CH)
            reads.append(pltpu.make_async_copy(src.at[where], stage.at[i, where], sem_in.at[i, c]))
            writes.append(pltpu.make_async_copy(stage.at[i, where], dst.at[where], sem_out.at[i, c]))
    reads.append(pltpu.make_async_copy(grad, small, sem_in.at[2, 0]))
    writes.append(pltpu.make_async_copy(small, grad_out, sem_out.at[2, 0]))
    for copy in reads:
        copy.start()
    for i in range(8):
        loss_out[pl.ds(i * 128, 128)] = loss[i, :]
    for read, write in zip(reads, writes):
        read.wait()
        write.start()
    for copy in writes:
        copy.wait()


def per_device(features, captions, head, scaling, offset, img, cap, cnt):
    hbm = pl.BlockSpec(memory_space=pl.ANY)
    smem = pl.BlockSpec(memory_space=pltpu.SMEM)
    vmem = pl.BlockSpec(memory_space=pltpu.VMEM)
    big = pltpu.VMEM((ROWS, D), BF)
    blocks = pltpu.VMEM((2, BLK, D), BF)
    dma = pltpu.SemaphoreType.DMA
    loss, pooled, text, grad = pl.pallas_call(
        kernel,
        out_shape=(
            jax.ShapeDtypeStruct((8, 128), F32),
            jax.ShapeDtypeStruct((ROWS, D), BF),
            jax.ShapeDtypeStruct((ROWS, D), BF),
            jax.ShapeDtypeStruct((HR, D), F32),
        ),
        in_specs=[hbm] * 3 + [smem] * 5,
        out_specs=(vmem, hbm, hbm, vmem),
        scratch_shapes=[
            big, big, big, blocks, blocks, pltpu.VMEM((D, D), BF), blocks, blocks,
            pltpu.VMEM((ROWS, D), F32), pltpu.VMEM((ROWS, D), F32), pltpu.VMEM((D, D), F32),
            big, big, big, big, pltpu.VMEM((10, BLK, BLK), BF), big,
            pltpu.VMEM((16, 2, HP, LO), BF), pltpu.VMEM((16, 2, HP, HI), BF),
            pltpu.VMEM((16, HP, LO), BF), pltpu.VMEM((16, HP, HI), BF),
            pltpu.VMEM((3, 4, HP, LO), BF), pltpu.VMEM((3, 4, HP, HI), BF),
            pltpu.VMEM((4, HP, LO), BF), pltpu.VMEM((4, HP, HI), BF),
            pltpu.VMEM((3, HP, LO), BF), pltpu.VMEM((3, HP, HI), BF),
            pltpu.VMEM((2, HP, D), BF), pltpu.VMEM((2, HP, D), BF),
            pltpu.VMEM((ROWS, 3), F32), pltpu.VMEM((2, BLK, 1), F32), pltpu.VMEM((2, BLK, 1), F32),
            pltpu.VMEM((8, 128), F32), pltpu.VMEM((8, 128), F32),
            dma((NSM,)), dma((NSM,)), dma((NSM,)), dma((NSM,)), dma((NCH,)), dma((NCH,)), dma((NCH,)), dma((NCH,)),
            dma((2,)), dma((4,)), dma((3, 4)), dma((3, 4)), dma((3,)), dma((3,)), dma((3,)), dma((3,)), dma((3,)), dma((3,)),
            dma((2,)), dma((2,)), dma((3,)), dma((2, NCH)),
        ],
        compiler_params=pltpu.CompilerParams(
            collective_id=0, has_side_effects=True, vmem_limit_bytes=63 << 20
        ),
        cost_estimate=pl.CostEstimate(flops=34_000_000_000, bytes_accessed=20_000_000, transcendentals=6_000_000),
    )(features, captions, head, scaling, offset, jnp.swapaxes(img, 2, 3), jnp.swapaxes(cap, 2, 3), cnt)
    return pl.pallas_call(
        emit,
        out_shape=(
            jax.ShapeDtypeStruct((ROWS,), F32),
            jax.ShapeDtypeStruct((ROWS, D), BF),
            jax.ShapeDtypeStruct((ROWS, D), BF),
            jax.ShapeDtypeStruct((HR, D), F32),
        ),
        in_specs=[vmem, hbm, hbm, hbm],
        out_specs=(vmem, hbm, hbm, hbm),
        scratch_shapes=[pltpu.VMEM((2, ROWS, D), BF), pltpu.VMEM((HR, D), F32), dma((3, NCH)), dma((3, NCH))],
        compiler_params=pltpu.CompilerParams(vmem_limit_bytes=63 << 20),
    )(loss, pooled, text, grad)


def solution(mesh):
    return jax.shard_map(
        per_device,
        mesh=mesh,
        in_specs=(
            P(("grp", "inner"), None),
            P(("grp", "inner"), None),
            P(),
            P(),
            P(),
            P(None, "inner", None, None),
            P(None, "inner", None, None),
            P(None, "inner", None),
        ),
        out_specs=(
            P(("grp", "inner")),
            P(("grp", "inner"), None),
            P(("grp", "inner"), None),
            P("inner", None),
        ),
        check_vma=False,
    )
```

```python
import functools

import jax
import jax.numpy as jnp
from jax import lax
from jax.experimental import pallas as pl
from jax.experimental.pallas import tpu as pltpu
from jax.sharding import PartitionSpec as P

MESH = pl.DeviceIdType.MESH
BLK = 512
D = 1152
ROWS = 1024
CH = 256
NCH = ROWS // CH
SM = 128
NSM = ROWS // SM
EPS = 1e-06
HR = 36
HP = 48
LO = 512
HI = D - LO
BF = jnp.bfloat16
F32 = jnp.float32

NN = (((1,), (0,)), ((), ()))
NT = (((1,), (1,)), ((), ()))
TN = (((0,), (0,)), ((), ()))


def mm(a, b, dims):
    return lax.dot_general(a, b, dims, preferred_element_type=F32)


def kernel(
    f_hbm, t_hbm, w_hbm, scale_ref, offset_ref, img_ref, cap_ref, cnt_ref,
    loss_out, iup, iun, head_out,
    fn, fp, tn, tun, tq, w, unit32, din, wide, si, st, ri, rt, gs, ep,
    hs_lo, hs_hi, rc_lo, rc_hi, rx, ry, ba, bb, r2a, r2b, zs, zr, inv, ls, lr,
    f_send, f_recv, t_send, t_recv, di_send, di_recv, dt_send, dt_recv,
    l_sem, c_sem, x_send, x_recv, y_send, y_recv, x2_send, x2_recv, y2_send, y2_recv,
    z_send, z_recv, in_sem,
):
    me = lax.axis_index("grp")
    inner = lax.axis_index("inner")
    odd = lax.rem(me, 2)
    gp = lax.rem(me + 3 + 2 * odd, 4)
    gq = lax.rem(me + 1 + 2 * odd, 4)
    core = lax.rem(inner, 2)
    x = lax.rem(inner // 2, 4)
    y = inner // 8

    def at(yy, xx, cc):
        return (yy * 4 + xx) * 2 + cc

    p_dev, q_dev = (gp, inner), (gq, inner)
    c_dev = (me, at(y, x, 1 - core))
    xs = [lax.rem(x + d, 4) for d in (1, 2, 3)]
    ys = [lax.rem(y + d, 4) for d in (1, 2, 3)]
    x_devs = [(me, at(y, v, core)) for v in xs]
    y_devs = [(me, at(v, x, core)) for v in ys]

    def remote(src, dst, send, recv, dev):
        return pltpu.make_async_remote_copy(
            src_ref=src, dst_ref=dst, send_sem=send, recv_sem=recv, device_id=dev, device_id_type=MESH
        )

    barrier = pltpu.get_barrier_semaphore()
    peers = [p_dev, q_dev, c_dev] + x_devs + y_devs
    for dev in peers:
        pl.semaphore_signal(barrier, inc=1, device_id=dev, device_id_type=MESH)
    pl.semaphore_wait(barrier, len(peers))

    def rows(c):
        return pl.ds(pl.multiple_of(c * CH, CH), CH)

    def half(c):
        return pl.ds(pl.multiple_of(lax.rem(c, 2) * CH, CH), CH)

    def small(c):
        return pl.ds(pl.multiple_of(c * SM, SM), SM)

    def part(c):
        return pl.ds(pl.multiple_of(lax.rem(c, 4) * SM, SM), SM)

    def f_copy(c):
        return remote(f_hbm.at[small(c)], fp.at[small(c)], f_send.at[c], f_recv.at[c], p_dev)

    def t_copy(c):
        return remote(t_hbm.at[small(c)], tq.at[c // 4, part(c)], t_send.at[c], t_recv.at[c], q_dev)

    def di_copy(c):
        return remote(si.at[small(c)], ri.at[small(c)], di_send.at[c], di_recv.at[c], p_dev)

    def dt_copy(c):
        return remote(st.at[small(c)], rt.at[small(c)], dt_send.at[c], dt_recv.at[c], q_dev)

    for c in range(NSM):
        f_copy(c).start()
        t_copy(c).start()
    w_in = pltpu.make_async_copy(w_hbm, w, in_sem.at[0])
    f_in = pltpu.make_async_copy(f_hbm, fn, in_sem.at[1])
    t_in = pltpu.make_async_copy(t_hbm, tn, in_sem.at[2])
    w_in.start()
    f_in.start()
    t_in.start()

    scale = scale_ref[0]
    offset = offset_ref[0]

    def pair(g, h):
        first = cap_ref[g, 0, 0, h]
        a0, a1, live = img_ref[g, 0, 0, h], img_ref[g, 0, 1, h], cnt_ref[g, 0, h]
        out = []
        for k in range(2):
            slot = jnp.abs(first - k)
            out.append((a0 + (a1 - a0) * slot, jnp.clip(live - slot, 0, 1).astype(F32)))
        return out

    pair_a, pair_b, pair_c = pair(gp, me), pair(me, gq), pair(gp, gq)

    def hit(sel, b):
        return (1 - jnp.abs(sel - b)).astype(F32)

    def norm(v):
        return lax.rsqrt(jnp.sum(v * v, axis=-1, keepdims=True) + EPS)

    def project(g, u, r):
        return (g - u * jnp.sum(g * u, axis=-1, keepdims=True)) * r

    def loop(n, body, start=0):
        lax.fori_loop(start, n, lambda i, _: (body(i), 0)[1], 0)

    def embed(f_ref, where):
        e = mm(f_ref[where, :], w[...], NN)
        r = norm(e)
        return e * r, r

    w_in.wait()
    f_in.wait()

    def embed_own(c):
        unit, r = embed(fn, rows(c))
        unit32[rows(c), :] = unit
        inv[rows(c), 0:1] = r
        iun[c // 2, half(c), :] = unit.astype(BF)

    loop(NCH, embed_own)
    t_in.wait()

    def text_own(c):
        v = tn[rows(c), :].astype(F32)
        r = norm(v)
        inv[rows(c), 2:3] = r
        tun[c // 2, half(c), :] = (v * r).astype(BF)

    loop(NCH, text_own)

    def line(b, start, n):
        return pl.ds(pl.multiple_of(b * BLK + start, SM), n)

    def tile(images, sel, texts, k, slot, live, diagonal):
        def body(r):
            s = mm(images[sel, half(r), :], texts[k], NT) * scale + offset
            if diagonal:
                on = (lax.broadcasted_iota(jnp.int32, s.shape, 0) + r * CH) == lax.broadcasted_iota(jnp.int32, s.shape, 1)
                s = jnp.where(on, -s, s)
            e = jnp.exp(s)
            g = e / (1.0 + e)
            if diagonal:
                g = jnp.where(on, -g, g)
            else:
                g = g * live
            gs[slot, half(r), :] = g.astype(BF)
            total = jnp.sum(jnp.log1p(e), axis=1, keepdims=True)
            return total

        return body

    def tile_diag(k):
        body = tile(iun, k, tun, k, k, None, True)

        def step(r):
            inv[line(k, r * CH, CH), 3:4] = body(r)

        loop(2, step)

    def tile_own(k, slot):
        sel, live = pair_b[k]
        body = tile(iun, sel, tq, k, slot, live, False)

        def step(r):
            total = body(r) * live
            for b in range(2):
                where = line(b, r * CH, CH)
                inv[where, 3:4] = inv[where, 3:4] + total * hit(sel, b)

        loop(2, step)

    def piece(b, r0, nr, k, c0, nc):
        sel, live = pair_c[k]
        keep = live * hit(sel, b)
        e = jnp.exp(mm(iup[b, r0 : r0 + nr, :], tq[k, c0 : c0 + nc, :], NT) * scale + offset)
        gs[8 + 2 * k + b, r0 : r0 + nr, c0 : c0 + nc] = (e / (1.0 + e) * keep).astype(BF)
        where = pl.ds(b * BLK + r0, nr)
        inv[where, 4:5] = inv[where, 4:5] + jnp.sum(jnp.log1p(e), axis=1, keepdims=True) * keep

    loop(2, tile_diag)

    def own_diag(c):
        b = c // 2
        din[rows(c), :] = mm(gs[b, half(c), :], tun[b], NN) * scale

    loop(NCH, own_diag)

    def arrive(c):
        b = c // 4
        f_copy(c).wait_recv()
        unit, r = embed(fp, small(c))
        wide[small(c), :] = unit
        inv[small(c), 1:2] = r
        u = unit.astype(BF)
        iup[b, part(c), :] = u
        total = None
        for k in range(2):
            sel, live = pair_a[k]
            keep = live * hit(sel, b)
            e = jnp.exp(mm(u, tun[k], NT) * scale + offset)
            gs[2 + 2 * k + b, part(c), :] = (e / (1.0 + e) * keep).astype(BF)
            v = jnp.sum(jnp.log1p(e), axis=1, keepdims=True) * keep
            total = v if total is None else total + v
        inv[small(c), 4:5] = total
        t_copy(c).wait_recv()
        v = tq[b, part(c), :].astype(F32)
        tq[b, part(c), :] = (v * norm(v)).astype(BF)

    loop(4, arrive)
    tile_own(0, 6)

    def back_text(c, parts):
        cols = half(c)
        out = None
        for slot, images, sel in parts:
            v = mm(gs[slot, :, cols], images[sel], TN)
            out = v if out is None else out + v
        return out * scale

    def back_image(c, parts):
        b = c // 2
        out = None
        for slot, texts, k, sel in parts:
            g = gs[slot, half(c), :]
            if sel is not None:
                g = (g.astype(F32) * hit(sel, b)).astype(BF)
            v = mm(g, texts[k], NN)
            out = v if out is None else out + v
        return out * scale

    def own_first(c):
        din[rows(c), :] = din[rows(c), :] + back_image(c, ((6, tq, 0, pair_b[0][0]),))

    loop(NCH, own_first)
    piece(0, 0, 256, 0, 0, 512)
    piece(0, 256, 256, 0, 0, 512)
    loop(6, arrive, 4)
    piece(1, 0, 256, 0, 0, 512)
    piece(1, 0, 256, 1, 0, 256)
    piece(0, 0, 512, 1, 0, 256)
    loop(7, arrive, 6)
    piece(1, 256, 128, 0, 0, 512)
    piece(1, 256, 128, 1, 0, 384)
    piece(0, 0, 512, 1, 256, 128)
    piece(1, 0, 256, 1, 256, 128)
    loop(NSM, arrive, 7)
    piece(1, 384, 128, 0, 0, 512)
    piece(1, 384, 128, 1, 0, 512)
    piece(0, 0, 512, 1, 384, 128)
    piece(1, 0, 384, 1, 384, 128)

    def send_text(c, last=False):
        k = c // 2
        sel_b = jnp.where(k == 0, pair_b[0][0], pair_b[1][0])
        sel_c = jnp.where(k == 0, pair_c[0][0], pair_c[1][0])
        st[rows(c), :] = back_text(c, ((6 + k, iun, sel_b), (8 + 2 * k + sel_c, iup, sel_c))).astype(BF)
        dt_copy(2 * c).start()
        if not last:
            dt_copy(2 * c + 1).start()

    def send_image(c, last=False):
        b = c // 2
        g = back_image(
            c,
            ((2 + b, tun, 0, None), (4 + b, tun, 1, None), (8 + b, tq, 0, None), (10 + b, tq, 1, None)),
        )
        si[rows(c), :] = g.astype(BF)
        di_copy(2 * c).start()
        if not last:
            di_copy(2 * c + 1).start()
        ep[rows(c), :] = project(g, wide[rows(c), :], inv[rows(c), 1:2]).astype(BF)

    loop(1, send_image)
    loop(1, send_text)
    loop(NCH - 1, send_image, 1)
    loop(NCH, lambda c: send_image(c, True), NCH - 1)
    loop(2, send_text, 1)

    def row_form(at_col, out):
        for i in range(8):
            v = inv[pl.ds(i * 128, 128), at_col : at_col + 1]
            out[pl.ds(i, 1), :] = jnp.transpose(jnp.broadcast_to(v, (128, 128)))[0:1, :]

    row_form(4, ls)
    l_copy = remote(ls, lr, l_sem.at[0], l_sem.at[1], p_dev)
    l_copy.start()
    tile_own(1, 7)

    def own_image(c):
        g = din[rows(c), :] + back_image(c, ((7, tq, 1, pair_b[1][0]),))
        din[rows(c), :] = g
        tun[c // 2, half(c), :] = project(g, unit32[rows(c), :], inv[rows(c), 0:1]).astype(BF)

    loop(NCH, own_image)

    def head(cols, hs, by_y):
        def step(j):
            own = pl.ds(pl.multiple_of(j * 384, 128), 384)
            h = mm(fp[:, own], ep[:, cols], TN)
            h = h + mm(fn[pl.ds(0, BLK), own], tun[0, :, cols], TN) + mm(fn[pl.ds(BLK, BLK), own], tun[1, :, cols], TN)
            wide[own, cols] = h

        loop(3, step)

        def split(j):
            v = []
            for i in range(4):
                at_row = (j * 4 + i if by_y else i * 4 + j) * 2 * HR
                v.append(wide[pl.ds(pl.multiple_of(at_row, 8), 2 * HR), cols])
            for c in range(2):
                hs[c, j] = jnp.concatenate([u[c * HR : (c + 1) * HR, :] for u in v], axis=0).astype(BF)

        loop(4, split)

    lo_cols, hi_cols = pl.ds(0, LO), pl.ds(LO, HI)
    head(lo_cols, hs_lo, False)
    c_lo = remote(hs_lo.at[1 - core], rc_lo, c_sem.at[0], c_sem.at[1], c_dev)
    c_lo.start()
    head(hi_cols, hs_hi, True)
    c_hi = remote(hs_hi.at[1 - core], rc_hi, c_sem.at[2], c_sem.at[3], c_dev)
    c_hi.start()
    loop(NCH - 1, send_text, 2)
    loop(NCH, lambda c: send_text(c, True), NCH - 1)

    def add_core(rc, hs):
        def step(j):
            rc[j] = (rc[j].astype(F32) + hs[core, j].astype(F32)).astype(BF)

        loop(4, step)

    c_lo.wait()
    add_core(rc_lo, hs_lo)
    xc = [remote(rc_lo.at[xs[d]], rx.at[d], x_send.at[d], x_recv.at[d], x_devs[d]) for d in range(3)]
    for copy in xc:
        copy.start()
    c_hi.wait()
    add_core(rc_hi, hs_hi)
    yc = [
        remote(rc_hi.at[ys[d]], ry.at[d], y_send.at[d], y_recv.at[d], y_devs[d]) for d in range(3)
    ]
    for copy in yc:
        copy.start()

    def own_text(c):
        b = c // 2
        sel = jnp.where(b == 0, pair_a[0][0], pair_a[1][0])
        v = mm(gs[b, :, half(c)], iun[b], TN) + mm(gs[2 + 2 * b + sel, :, half(c)], iup[sel], TN)
        wide[rows(c), :] = v * scale

    loop(NCH, own_text)

    def finish(c, n=CH):
        where = pl.ds(pl.multiple_of(c * n, SM), n)
        inside = pl.ds(pl.multiple_of(lax.rem(c, BLK // n) * n, SM), n)
        b = c // (BLK // n)
        for i in range(n // SM):
            di_copy(c * (n // SM) + i).wait_recv()
        g = din[where, :] + ri[where, :].astype(F32)
        eg = project(g, unit32[where, :], inv[where, 0:1]).astype(BF)
        iup[b, inside, :] = mm(eg, w[...], NT).astype(BF)
        for i in range(n // SM):
            dt_copy(c * (n // SM) + i).wait_recv()
        u = tn[where, :].astype(F32) * inv[where, 2:3]
        gt = wide[where, :] + rt[where, :].astype(F32)
        iun[b, inside, :] = project(gt, u, inv[where, 2:3]).astype(BF)

    loop(2, finish)

    def fold(rc, mine, recv, out):
        v = rc[mine].astype(F32)
        for d in range(3):
            v = v + recv[d].astype(F32)
        zero = jnp.zeros((HP - HR, v.shape[1]), F32)
        for i in range(4):
            out[i] = jnp.concatenate([v[i * HR : (i + 1) * HR, :], zero], axis=0).astype(BF)

    for copy in xc:
        copy.wait()
    fold(rc_lo, x, rx, ba)
    second = [remote(ba.at[ys[d]], r2a.at[d], y2_send.at[d], y2_recv.at[d], y_devs[d]) for d in range(3)]
    for copy in second:
        copy.start()
    for copy in yc:
        copy.wait()
    fold(rc_hi, y, ry, bb)
    third = [remote(bb.at[xs[d]], r2b.at[d], x2_send.at[d], x2_recv.at[d], x_devs[d]) for d in range(3)]
    for copy in third:
        copy.start()
    loop(3, finish, 2)
    for copy in second + third:
        copy.wait()
    lo = ba[y].astype(F32)
    hi = bb[x].astype(F32)
    for d in range(3):
        lo = lo + r2a[d].astype(F32)
        hi = hi + r2b[d].astype(F32)
    zs[0, :, pl.ds(0, LO)] = lo.astype(BF)
    zs[0, :, pl.ds(LO, HI)] = hi.astype(BF)
    z0 = remote(zs.at[0], zr.at[0], z_send.at[0], z_recv.at[0], p_dev)
    z0.start()
    di_copy(NSM - 1).start()
    z0.wait()
    zs[1] = (zs[0].astype(F32) + zr[0].astype(F32)).astype(BF)
    z1 = remote(zs.at[1], zr.at[1], z_send.at[1], z_recv.at[1], q_dev)
    z1.start()
    dt_copy(NSM - 1).start()
    loop(NSM - 1, lambda c: finish(c, SM), NSM - 2)
    loop(NSM, lambda c: finish(c, SM), NSM - 1)
    l_copy.wait()
    row_form(3, ls)
    loss_out[...] = (ls[...] + lr[...]) * (1.0 / BLK)
    z1.wait()
    head_out[...] = (zs[1].astype(F32) + zr[1].astype(F32))[0:HR, :]

    def sent(c):
        f_copy(c).wait_send()
        t_copy(c).wait_send()
        di_copy(c).wait_send()
        dt_copy(c).wait_send()

    loop(NSM, sent)


def emit(loss, pooled, text, grad, loss_out, pooled_out, text_out, grad_out, sem):
    pairs = ((pooled, pooled_out), (text, text_out), (grad, grad_out))
    copies = [pltpu.make_async_copy(a, b, sem.at[i]) for i, (a, b) in enumerate(pairs)]
    for copy in copies:
        copy.start()
    for i in range(8):
        loss_out[pl.ds(i * 128, 128)] = loss[i, :]
    for copy in copies:
        copy.wait()


def per_device(features, captions, head, scaling, offset, img, cap, cnt):
    hbm = pl.BlockSpec(memory_space=pl.ANY)
    smem = pl.BlockSpec(memory_space=pltpu.SMEM)
    vmem = pl.BlockSpec(memory_space=pltpu.VMEM)
    big = pltpu.VMEM((ROWS, D), BF)
    blocks = pltpu.VMEM((2, BLK, D), BF)
    dma = pltpu.SemaphoreType.DMA
    loss, pooled, text, grad = pl.pallas_call(
        kernel,
        out_shape=(pltpu.VMEM((8, 128), F32), blocks, blocks, pltpu.VMEM((HR, D), F32)),
        in_specs=[hbm] * 3 + [smem] * 5,
        out_specs=(vmem, vmem, vmem, vmem),
        scratch_shapes=[
            big, big, big, blocks, blocks, pltpu.VMEM((D, D), BF),
            pltpu.VMEM((ROWS, D), F32), pltpu.VMEM((ROWS, D), F32), pltpu.VMEM((D, D), F32),
            big, big, big, big, pltpu.VMEM((12, BLK, BLK), BF), big,
            pltpu.VMEM((2, 4, 4 * HR, LO), BF), pltpu.VMEM((2, 4, 4 * HR, HI), BF),
            pltpu.VMEM((4, 4 * HR, LO), BF), pltpu.VMEM((4, 4 * HR, HI), BF),
            pltpu.VMEM((3, 4 * HR, LO), BF), pltpu.VMEM((3, 4 * HR, HI), BF),
            pltpu.VMEM((4, HP, LO), BF), pltpu.VMEM((4, HP, HI), BF),
            pltpu.VMEM((3, HP, LO), BF), pltpu.VMEM((3, HP, HI), BF),
            pltpu.VMEM((2, HP, D), BF), pltpu.VMEM((2, HP, D), BF),
            pltpu.VMEM((ROWS, 5), F32),
            pltpu.VMEM((8, 128), F32), pltpu.VMEM((8, 128), F32),
            dma((NSM,)), dma((NSM,)), dma((NSM,)), dma((NSM,)), dma((NSM,)), dma((NSM,)), dma((NSM,)), dma((NSM,)),
            dma((2,)), dma((4,)), dma((3,)), dma((3,)), dma((3,)), dma((3,)), dma((3,)), dma((3,)), dma((3,)), dma((3,)),
            dma((2,)), dma((2,)), dma((3,)),
        ],
        compiler_params=pltpu.CompilerParams(
            collective_id=0, has_side_effects=True, vmem_limit_bytes=57 << 20
        ),
        cost_estimate=pl.CostEstimate(flops=34_000_000_000, bytes_accessed=20_000_000, transcendentals=6_000_000),
    )(features, captions, head, scaling, offset, jnp.swapaxes(img, 2, 3), jnp.swapaxes(cap, 2, 3), cnt)
    loss, pooled, text, grad = pl.pallas_call(
        emit,
        out_shape=(
            jax.ShapeDtypeStruct((ROWS,), F32),
            jax.ShapeDtypeStruct((2, BLK, D), BF),
            jax.ShapeDtypeStruct((2, BLK, D), BF),
            jax.ShapeDtypeStruct((HR, D), F32),
        ),
        in_specs=[vmem, hbm, hbm, hbm],
        out_specs=(vmem, hbm, hbm, hbm),
        scratch_shapes=[dma((3,))],
        compiler_params=pltpu.CompilerParams(vmem_limit_bytes=4 << 20),
    )(*(pltpu.with_memory_space_constraint(v, pltpu.VMEM) for v in (loss, pooled, text, grad)))
    return loss, pooled.reshape(ROWS, D), text.reshape(ROWS, D), grad


def solution(mesh):
    return jax.shard_map(
        per_device,
        mesh=mesh,
        in_specs=(
            P(("grp", "inner"), None),
            P(("grp", "inner"), None),
            P(),
            P(),
            P(),
            P(None, "inner", None, None),
            P(None, "inner", None, None),
            P(None, "inner", None),
        ),
        out_specs=(
            P(("grp", "inner")),
            P(("grp", "inner"), None),
            P(("grp", "inner"), None),
            P("inner", None),
        ),
        check_vma=False,
    )
```

```python
import functools

import jax
import jax.numpy as jnp
from jax import lax
from jax.experimental import pallas as pl
from jax.experimental.pallas import tpu as pltpu
from jax.sharding import PartitionSpec as P

MESH = pl.DeviceIdType.MESH
BLK = 512
D = 1152
ROWS = 1024
CH = 256
NCH = ROWS // CH
SM = 128
NSM = ROWS // SM
EPS = 1e-06
HR = 36
HP = 48
LO = 640
HI = D - LO
BF = jnp.bfloat16
F32 = jnp.float32

NN = (((1,), (0,)), ((), ()))
NT = (((1,), (1,)), ((), ()))
TN = (((0,), (0,)), ((), ()))


def mm(a, b, dims):
    return lax.dot_general(a, b, dims, preferred_element_type=F32)


def kernel(
    f_hbm, t_hbm, w_hbm, scale_ref, offset_ref, img_hbm, cap_hbm, cnt_hbm,
    loss_out, iup, iun, head_out,
    img_ref, cap_ref, cnt_ref,
    fn, fp, tn, tun, tq, w, unit32, din, wide, si, st, ri, rt, gs, ep,
    hs_lo, hs_hi, rc_lo, rc_hi, rx, ry, ba, bb, r2a, r2b, zs, zr, inv, ls, lr,
    f_send, f_recv, t_send, t_recv, di_send, di_recv, dt_send, dt_recv,
    l_sem, c_sem, x_send, x_recv, y_send, y_recv, x2_send, x2_recv, y2_send, y2_recv,
    z_send, z_recv, in_sem,
):
    me = lax.axis_index("grp")
    inner = lax.axis_index("inner")
    odd = lax.rem(me, 2)
    gp = lax.rem(me + 3 + 2 * odd, 4)
    gq = lax.rem(me + 1 + 2 * odd, 4)
    core = lax.rem(inner, 2)
    x = lax.rem(inner // 2, 4)
    y = inner // 8

    def at(yy, xx, cc):
        return (yy * 4 + xx) * 2 + cc

    p_dev, q_dev = (gp, inner), (gq, inner)
    c_dev = (me, at(y, x, 1 - core))
    xs = [lax.rem(x + d, 4) for d in (1, 2, 3)]
    ys = [lax.rem(y + d, 4) for d in (1, 2, 3)]
    x_devs = [(me, at(y, v, core)) for v in xs]
    y_devs = [(me, at(v, x, core)) for v in ys]

    def remote(src, dst, send, recv, dev):
        return pltpu.make_async_remote_copy(
            src_ref=src, dst_ref=dst, send_sem=send, recv_sem=recv, device_id=dev, device_id_type=MESH
        )

    scalars = [
        pltpu.make_async_copy(src, dst, in_sem.at[3 + i])
        for i, (src, dst) in enumerate(((img_hbm, img_ref), (cap_hbm, cap_ref), (cnt_hbm, cnt_ref)))
    ]
    for copy in scalars:
        copy.start()
    barrier = pltpu.get_barrier_semaphore()
    peers = [p_dev, q_dev, c_dev] + x_devs + y_devs
    for dev in peers:
        pl.semaphore_signal(barrier, inc=1, device_id=dev, device_id_type=MESH)
    pl.semaphore_wait(barrier, len(peers))

    def rows(c):
        return pl.ds(pl.multiple_of(c * CH, CH), CH)

    def half(c):
        return pl.ds(pl.multiple_of(lax.rem(c, 2) * CH, CH), CH)

    def small(c):
        return pl.ds(pl.multiple_of(c * SM, SM), SM)

    def part(c):
        return pl.ds(pl.multiple_of(lax.rem(c, 4) * SM, SM), SM)

    def f_copy(c):
        return remote(f_hbm.at[small(c)], fp.at[small(c)], f_send.at[c], f_recv.at[c], p_dev)

    def t_copy(c):
        return remote(t_hbm.at[small(c)], tq.at[c // 4, part(c)], t_send.at[c], t_recv.at[c], q_dev)

    def di_copy(c):
        return remote(si.at[small(c)], ri.at[small(c)], di_send.at[c], di_recv.at[c], p_dev)

    def dt_copy(c):
        return remote(st.at[small(c)], rt.at[small(c)], dt_send.at[c], dt_recv.at[c], q_dev)

    for c in range(NSM):
        f_copy(c).start()
        t_copy(c).start()
    w_in = pltpu.make_async_copy(w_hbm, w, in_sem.at[0])
    f_in = pltpu.make_async_copy(f_hbm, fn, in_sem.at[1])
    t_in = pltpu.make_async_copy(t_hbm, tn, in_sem.at[2])
    w_in.start()
    f_in.start()
    t_in.start()

    for copy in scalars:
        copy.wait()
    scale = scale_ref[0]
    offset = offset_ref[0]

    def pair(g, h):
        first = cap_ref[g, 0, 0, h]
        a0, a1, live = img_ref[g, 0, 0, h], img_ref[g, 0, 1, h], cnt_ref[g, 0, h]
        out = []
        for k in range(2):
            slot = jnp.abs(first - k)
            out.append((a0 + (a1 - a0) * slot, jnp.clip(live - slot, 0, 1).astype(F32)))
        return out

    pair_a, pair_b, pair_c = pair(gp, me), pair(me, gq), pair(gp, gq)

    def hit(sel, b):
        return (1 - jnp.abs(sel - b)).astype(F32)

    def norm(v):
        return lax.rsqrt(jnp.sum(v * v, axis=-1, keepdims=True) + EPS)

    def project(g, u, r):
        return (g - u * jnp.sum(g * u, axis=-1, keepdims=True)) * r

    def loop(n, body, start=0):
        lax.fori_loop(start, n, lambda i, _: (body(i), 0)[1], 0)

    def embed(f_ref, where):
        e = mm(f_ref[where, :], w[...], NN)
        r = norm(e)
        return e * r, r

    w_in.wait()
    f_in.wait()

    def embed_own(c):
        unit, r = embed(fn, rows(c))
        unit32[rows(c), :] = unit
        inv[rows(c), 0:1] = r
        iun[c // 2, half(c), :] = unit.astype(BF)

    loop(NCH, embed_own)
    t_in.wait()

    def text_own(c):
        v = tn[rows(c), :].astype(F32)
        r = norm(v)
        inv[rows(c), 2:3] = r
        tun[c // 2, half(c), :] = (v * r).astype(BF)

    loop(NCH, text_own)

    def line(b, start, n):
        return pl.ds(pl.multiple_of(b * BLK + start, SM), n)

    def tile(images, sel, texts, k, slot, live, diagonal):
        def body(r):
            s = mm(images[sel, half(r), :], texts[k], NT) * scale + offset
            if diagonal:
                on = (lax.broadcasted_iota(jnp.int32, s.shape, 0) + r * CH) == lax.broadcasted_iota(jnp.int32, s.shape, 1)
                s = jnp.where(on, -s, s)
            e = jnp.exp(s)
            g = e / (1.0 + e)
            if diagonal:
                g = jnp.where(on, -g, g)
            else:
                g = g * live
            gs[slot, half(r), :] = g.astype(BF)
            total = jnp.sum(jnp.log1p(e), axis=1, keepdims=True)
            return total

        return body

    def tile_diag(k):
        body = tile(iun, k, tun, k, k, None, True)

        def step(r):
            inv[line(k, r * CH, CH), 3:4] = body(r)

        loop(2, step)

    def tile_own(k, slot):
        sel, live = pair_b[k]
        body = tile(iun, sel, tq, k, slot, live, False)

        def step(r):
            total = body(r) * live
            for b in range(2):
                where = line(b, r * CH, CH)
                inv[where, 3:4] = inv[where, 3:4] + total * hit(sel, b)

        loop(2, step)

    def piece(b, r0, nr, k, c0, nc):
        sel, live = pair_c[k]
        keep = live * hit(sel, b)
        e = jnp.exp(mm(iup[b, r0 : r0 + nr, :], tq[k, c0 : c0 + nc, :], NT) * scale + offset)
        gs[8 + 2 * k + b, r0 : r0 + nr, c0 : c0 + nc] = (e / (1.0 + e) * keep).astype(BF)
        where = pl.ds(b * BLK + r0, nr)
        inv[where, 4:5] = inv[where, 4:5] + jnp.sum(jnp.log1p(e), axis=1, keepdims=True) * keep

    loop(2, tile_diag)

    def own_diag(c):
        b = c // 2
        din[rows(c), :] = mm(gs[b, half(c), :], tun[b], NN) * scale

    loop(NCH, own_diag)

    def arrive(c):
        b = c // 4
        f_copy(c).wait_recv()
        unit, r = embed(fp, small(c))
        wide[small(c), :] = unit
        inv[small(c), 1:2] = r
        u = unit.astype(BF)
        iup[b, part(c), :] = u
        total = None
        for k in range(2):
            sel, live = pair_a[k]
            keep = live * hit(sel, b)
            e = jnp.exp(mm(u, tun[k], NT) * scale + offset)
            gs[2 + 2 * k + b, part(c), :] = (e / (1.0 + e) * keep).astype(BF)
            v = jnp.sum(jnp.log1p(e), axis=1, keepdims=True) * keep
            total = v if total is None else total + v
        inv[small(c), 4:5] = total
        t_copy(c).wait_recv()
        v = tq[b, part(c), :].astype(F32)
        tq[b, part(c), :] = (v * norm(v)).astype(BF)

    loop(4, arrive)
    tile_own(0, 6)

    def back_text(c, parts):
        cols = half(c)
        out = None
        for slot, images, sel in parts:
            v = mm(gs[slot, :, cols], images[sel], TN)
            out = v if out is None else out + v
        return out * scale

    def back_image(c, parts):
        b = c // 2
        out = None
        for slot, texts, k, sel in parts:
            g = gs[slot, half(c), :]
            if sel is not None:
                g = (g.astype(F32) * hit(sel, b)).astype(BF)
            v = mm(g, texts[k], NN)
            out = v if out is None else out + v
        return out * scale

    def own_first(c):
        din[rows(c), :] = din[rows(c), :] + back_image(c, ((6, tq, 0, pair_b[0][0]),))

    loop(NCH, own_first)
    piece(0, 0, 256, 0, 0, 512)
    piece(0, 256, 256, 0, 0, 512)
    loop(6, arrive, 4)
    piece(1, 0, 256, 0, 0, 512)
    piece(1, 0, 256, 1, 0, 256)
    piece(0, 0, 512, 1, 0, 256)
    loop(7, arrive, 6)
    piece(1, 256, 128, 0, 0, 512)
    piece(1, 256, 128, 1, 0, 384)
    piece(0, 0, 512, 1, 256, 128)
    piece(1, 0, 256, 1, 256, 128)
    loop(NSM, arrive, 7)
    piece(1, 384, 128, 0, 0, 512)
    piece(1, 384, 128, 1, 0, 512)
    piece(0, 0, 512, 1, 384, 128)
    piece(1, 0, 384, 1, 384, 128)

    def send_text(c):
        k = c // 2
        sel_b = jnp.where(k == 0, pair_b[0][0], pair_b[1][0])
        sel_c = jnp.where(k == 0, pair_c[0][0], pair_c[1][0])
        st[rows(c), :] = back_text(c, ((6 + k, iun, sel_b), (8 + 2 * k + sel_c, iup, sel_c))).astype(BF)
        dt_copy(2 * c).start()
        dt_copy(2 * c + 1).start()

    def send_image(c, last=False):
        b = c // 2
        g = back_image(
            c,
            ((2 + b, tun, 0, None), (4 + b, tun, 1, None), (8 + b, tq, 0, None), (10 + b, tq, 1, None)),
        )
        si[rows(c), :] = g.astype(BF)
        di_copy(2 * c).start()
        if not last:
            di_copy(2 * c + 1).start()
        ep[rows(c), :] = project(g, wide[rows(c), :], inv[rows(c), 1:2]).astype(BF)

    loop(1, send_image)
    loop(1, send_text)
    loop(NCH - 1, send_image, 1)
    loop(NCH, lambda c: send_image(c, True), NCH - 1)
    loop(2, send_text, 1)

    def row_form(at_col, out):
        for i in range(8):
            v = inv[pl.ds(i * 128, 128), at_col : at_col + 1]
            out[pl.ds(i, 1), :] = jnp.transpose(jnp.broadcast_to(v, (128, 128)))[0:1, :]

    row_form(4, ls)
    l_copy = remote(ls, lr, l_sem.at[0], l_sem.at[1], p_dev)
    l_copy.start()
    tile_own(1, 7)

    def own_image(c):
        g = din[rows(c), :] + back_image(c, ((7, tq, 1, pair_b[1][0]),))
        din[rows(c), :] = g
        tun[c // 2, half(c), :] = project(g, unit32[rows(c), :], inv[rows(c), 0:1]).astype(BF)

    loop(NCH, own_image)

    def head(cols, hs, by_y):
        def step(j):
            own = pl.ds(pl.multiple_of(j * 384, 128), 384)
            h = mm(fp[:, own], ep[:, cols], TN)
            h = h + mm(fn[pl.ds(0, BLK), own], tun[0, :, cols], TN) + mm(fn[pl.ds(BLK, BLK), own], tun[1, :, cols], TN)
            wide[own, cols] = h

        loop(3, step)

        def split(j):
            v = []
            for i in range(4):
                at_row = (j * 4 + i if by_y else i * 4 + j) * 2 * HR
                v.append(wide[pl.ds(pl.multiple_of(at_row, 8), 2 * HR), cols])
            for c in range(2):
                hs[c, j] = jnp.concatenate([u[c * HR : (c + 1) * HR, :] for u in v], axis=0).astype(BF)

        loop(4, split)

    lo_cols, hi_cols = pl.ds(0, LO), pl.ds(LO, HI)
    head(lo_cols, hs_lo, False)
    c_lo = remote(hs_lo.at[1 - core], rc_lo, c_sem.at[0], c_sem.at[1], c_dev)
    c_lo.start()
    head(hi_cols, hs_hi, True)
    c_hi = remote(hs_hi.at[1 - core], rc_hi, c_sem.at[2], c_sem.at[3], c_dev)
    c_hi.start()

    def add_core(rc, hs):
        def step(j):
            rc[j] = (rc[j].astype(F32) + hs[core, j].astype(F32)).astype(BF)

        loop(4, step)

    c_lo.wait()
    add_core(rc_lo, hs_lo)
    xc = [remote(rc_lo.at[xs[d]], rx.at[d], x_send.at[d], x_recv.at[d], x_devs[d]) for d in range(3)]
    for copy in xc:
        copy.start()
    loop(NCH, send_text, 2)
    c_hi.wait()
    add_core(rc_hi, hs_hi)
    yc = [
        remote(rc_hi.at[ys[d]], ry.at[d], y_send.at[d], y_recv.at[d], y_devs[d]) for d in range(3)
    ]
    for copy in yc:
        copy.start()

    def own_text(c):
        b = c // 2
        sel = jnp.where(b == 0, pair_a[0][0], pair_a[1][0])
        v = mm(gs[b, :, half(c)], iun[b], TN) + mm(gs[2 + 2 * b + sel, :, half(c)], iup[sel], TN)
        wide[rows(c), :] = v * scale

    loop(NCH, own_text)

    def finish(c, n=CH):
        where = pl.ds(pl.multiple_of(c * n, SM), n)
        inside = pl.ds(pl.multiple_of(lax.rem(c, BLK // n) * n, SM), n)
        b = c // (BLK // n)
        for i in range(n // SM):
            di_copy(c * (n // SM) + i).wait_recv()
        g = din[where, :] + ri[where, :].astype(F32)
        eg = project(g, unit32[where, :], inv[where, 0:1]).astype(BF)
        iup[b, inside, :] = mm(eg, w[...], NT).astype(BF)
        for i in range(n // SM):
            dt_copy(c * (n // SM) + i).wait_recv()
        u = tn[where, :].astype(F32) * inv[where, 2:3]
        gt = wide[where, :] + rt[where, :].astype(F32)
        iun[b, inside, :] = project(gt, u, inv[where, 2:3]).astype(BF)

    loop(2, finish)

    def fold(rc, mine, recv, out):
        v = rc[mine].astype(F32)
        for d in range(3):
            v = v + recv[d].astype(F32)
        zero = jnp.zeros((HP - HR, v.shape[1]), F32)
        for i in range(4):
            out[i] = jnp.concatenate([v[i * HR : (i + 1) * HR, :], zero], axis=0).astype(BF)

    for copy in xc:
        copy.wait()
    fold(rc_lo, x, rx, ba)
    second = [remote(ba.at[ys[d]], r2a.at[d], y2_send.at[d], y2_recv.at[d], y_devs[d]) for d in range(3)]
    for copy in second:
        copy.start()
    for copy in yc:
        copy.wait()
    fold(rc_hi, y, ry, bb)
    third = [remote(bb.at[xs[d]], r2b.at[d], x2_send.at[d], x2_recv.at[d], x_devs[d]) for d in range(3)]
    for copy in third:
        copy.start()
    loop(3, finish, 2)
    for copy in second + third:
        copy.wait()
    lo = ba[y].astype(F32)
    hi = bb[x].astype(F32)
    for d in range(3):
        lo = lo + r2a[d].astype(F32)
        hi = hi + r2b[d].astype(F32)
    zs[0, :, pl.ds(0, LO)] = lo.astype(BF)
    zs[0, :, pl.ds(LO, HI)] = hi.astype(BF)
    z0 = remote(zs.at[0], zr.at[0], z_send.at[0], z_recv.at[0], p_dev)
    z0.start()
    di_copy(NSM - 1).start()
    z0.wait()
    zs[1] = (zs[0].astype(F32) + zr[0].astype(F32)).astype(BF)
    z1 = remote(zs.at[1], zr.at[1], z_send.at[1], z_recv.at[1], q_dev)
    z1.start()
    loop(NSM - 1, lambda c: finish(c, SM), NSM - 2)
    loop(NSM, lambda c: finish(c, SM), NSM - 1)
    l_copy.wait()
    row_form(3, ls)
    loss_out[...] = (ls[...] + lr[...]) * (1.0 / BLK)
    z1.wait()
    head_out[...] = (zs[1].astype(F32) + zr[1].astype(F32))[0:HR, :]

    def sent(c):
        f_copy(c).wait_send()
        t_copy(c).wait_send()
        di_copy(c).wait_send()
        dt_copy(c).wait_send()

    loop(NSM, sent)


def emit(loss, pooled, text, grad, loss_out, pooled_out, text_out, grad_out, sem):
    copies = [pltpu.make_async_copy(grad, grad_out, sem.at[8])]
    for i in range(4):
        where = pl.ds(i % 2 * CH, CH)
        copies.append(pltpu.make_async_copy(pooled.at[i // 2, where], pooled_out.at[i // 2, where], sem.at[i]))
        copies.append(pltpu.make_async_copy(text.at[i // 2, where], text_out.at[i // 2, where], sem.at[4 + i]))
    for copy in copies:
        copy.start()
    for i in range(8):
        loss_out[pl.ds(i * 128, 128)] = loss[i, :]
    for copy in copies:
        copy.wait()


def per_device(features, captions, head, scaling, offset, img, cap, cnt):
    hbm = pl.BlockSpec(memory_space=pl.ANY)
    smem = pl.BlockSpec(memory_space=pltpu.SMEM)
    vmem = pl.BlockSpec(memory_space=pltpu.VMEM)
    big = pltpu.VMEM((ROWS, D), BF)
    blocks = pltpu.VMEM((2, BLK, D), BF)
    dma = pltpu.SemaphoreType.DMA
    loss, pooled, text, grad = pl.pallas_call(
        kernel,
        out_shape=(pltpu.VMEM((8, 128), F32), blocks, blocks, pltpu.VMEM((HR, D), F32)),
        in_specs=[hbm] * 3 + [smem] * 2 + [hbm] * 3,
        out_specs=(vmem, vmem, vmem, vmem),
        scratch_shapes=[
            pltpu.SMEM((4, 1, 2, 4), jnp.int32), pltpu.SMEM((4, 1, 2, 4), jnp.int32), pltpu.SMEM((4, 1, 4), jnp.int32),
            big, big, big, blocks, blocks, pltpu.VMEM((D, D), BF),
            pltpu.VMEM((ROWS, D), F32), pltpu.VMEM((ROWS, D), F32), pltpu.VMEM((D, D), F32),
            big, big, big, big, pltpu.VMEM((12, BLK, BLK), BF), big,
            pltpu.VMEM((2, 4, 4 * HR, LO), BF), pltpu.VMEM((2, 4, 4 * HR, HI), BF),
            pltpu.VMEM((4, 4 * HR, LO), BF), pltpu.VMEM((4, 4 * HR, HI), BF),
            pltpu.VMEM((3, 4 * HR, LO), BF), pltpu.VMEM((3, 4 * HR, HI), BF),
            pltpu.VMEM((4, HP, LO), BF), pltpu.VMEM((4, HP, HI), BF),
            pltpu.VMEM((3, HP, LO), BF), pltpu.VMEM((3, HP, HI), BF),
            pltpu.VMEM((2, HP, D), BF), pltpu.VMEM((2, HP, D), BF),
            pltpu.VMEM((ROWS, 5), F32),
            pltpu.VMEM((8, 128), F32), pltpu.VMEM((8, 128), F32),
            dma((NSM,)), dma((NSM,)), dma((NSM,)), dma((NSM,)), dma((NSM,)), dma((NSM,)), dma((NSM,)), dma((NSM,)),
            dma((2,)), dma((4,)), dma((3,)), dma((3,)), dma((3,)), dma((3,)), dma((3,)), dma((3,)), dma((3,)), dma((3,)),
            dma((2,)), dma((2,)), dma((6,)),
        ],
        compiler_params=pltpu.CompilerParams(
            collective_id=0, has_side_effects=True, vmem_limit_bytes=57 << 20
        ),
        cost_estimate=pl.CostEstimate(flops=34_000_000_000, bytes_accessed=20_000_000, transcendentals=6_000_000),
    )(features, captions, head, scaling, offset, jnp.swapaxes(img, 2, 3), jnp.swapaxes(cap, 2, 3), cnt)
    loss, pooled, text, grad = pl.pallas_call(
        emit,
        out_shape=(
            jax.ShapeDtypeStruct((ROWS,), F32),
            jax.ShapeDtypeStruct((2, BLK, D), BF),
            jax.ShapeDtypeStruct((2, BLK, D), BF),
            jax.ShapeDtypeStruct((HR, D), F32),
        ),
        in_specs=[vmem, hbm, hbm, hbm],
        out_specs=(vmem, hbm, hbm, hbm),
        scratch_shapes=[dma((9,))],
        compiler_params=pltpu.CompilerParams(vmem_limit_bytes=4 << 20),
    )(*(pltpu.with_memory_space_constraint(v, pltpu.VMEM) for v in (loss, pooled, text, grad)))
    return loss, pooled.reshape(ROWS, D), text.reshape(ROWS, D), grad


def solution(mesh):
    return jax.shard_map(
        per_device,
        mesh=mesh,
        in_specs=(
            P(("grp", "inner"), None),
            P(("grp", "inner"), None),
            P(),
            P(),
            P(),
            P(None, "inner", None, None),
            P(None, "inner", None, None),
            P(None, "inner", None),
        ),
        out_specs=(
            P(("grp", "inner")),
            P(("grp", "inner"), None),
            P(("grp", "inner"), None),
            P("inner", None),
        ),
        check_vma=False,
    )
```

```python
import functools

import jax
import jax.numpy as jnp
from jax import lax
from jax.experimental import pallas as pl
from jax.experimental.pallas import tpu as pltpu
from jax.sharding import PartitionSpec as P

MESH = pl.DeviceIdType.MESH
BLK = 512
D = 1152
ROWS = 1024
CH = 256
NCH = ROWS // CH
SM = 128
NSM = ROWS // SM
EPS = 1e-06
HR = 36
HP = 48
LO = 640
HI = D - LO
BF = jnp.bfloat16
F32 = jnp.float32

NN = (((1,), (0,)), ((), ()))
NT = (((1,), (1,)), ((), ()))
TN = (((0,), (0,)), ((), ()))


def mm(a, b, dims):
    return lax.dot_general(a, b, dims, preferred_element_type=F32)


def kernel(
    f_hbm, t_hbm, w_hbm, scale_ref, offset_ref, img_hbm, cap_hbm, cnt_hbm,
    loss_out, iup, iun, head_out,
    img_ref, cap_ref, cnt_ref,
    fn, fp, tn, tun, tq, w, unit32, din, wide, si, st, ri, rt, gs, ep,
    hs_lo, hs_hi, rc_lo, rc_hi, rx, ry, ba, bb, r2a, r2b, zs, zr, inv, ls, lr,
    f_send, f_recv, t_send, t_recv, di_send, di_recv, dt_send, dt_recv,
    l_sem, c_sem, x_send, x_recv, y_send, y_recv, x2_send, x2_recv, y2_send, y2_recv,
    z_send, z_recv, in_sem,
):
    me = lax.axis_index("grp")
    inner = lax.axis_index("inner")
    odd = lax.rem(me, 2)
    gp = lax.rem(me + 3 + 2 * odd, 4)
    gq = lax.rem(me + 1 + 2 * odd, 4)
    core = lax.rem(inner, 2)
    x = lax.rem(inner // 2, 4)
    y = inner // 8

    def at(yy, xx, cc):
        return (yy * 4 + xx) * 2 + cc

    p_dev, q_dev = (gp, inner), (gq, inner)
    c_dev = (me, at(y, x, 1 - core))
    xs = [lax.rem(x + d, 4) for d in (1, 2, 3)]
    ys = [lax.rem(y + d, 4) for d in (1, 2, 3)]
    x_devs = [(me, at(y, v, core)) for v in xs]
    y_devs = [(me, at(v, x, core)) for v in ys]

    def remote(src, dst, send, recv, dev):
        return pltpu.make_async_remote_copy(
            src_ref=src, dst_ref=dst, send_sem=send, recv_sem=recv, device_id=dev, device_id_type=MESH
        )

    scalars = [
        pltpu.make_async_copy(src, dst, in_sem.at[3 + i])
        for i, (src, dst) in enumerate(((img_hbm, img_ref), (cap_hbm, cap_ref), (cnt_hbm, cnt_ref)))
    ]
    for copy in scalars:
        copy.start()
    barrier = pltpu.get_barrier_semaphore()
    peers = [p_dev, q_dev, c_dev] + x_devs + y_devs
    for dev in peers:
        pl.semaphore_signal(barrier, inc=1, device_id=dev, device_id_type=MESH)
    pl.semaphore_wait(barrier, len(peers))

    def rows(c):
        return pl.ds(pl.multiple_of(c * CH, CH), CH)

    def half(c):
        return pl.ds(pl.multiple_of(lax.rem(c, 2) * CH, CH), CH)

    def small(c):
        return pl.ds(pl.multiple_of(c * SM, SM), SM)

    def part(c):
        return pl.ds(pl.multiple_of(lax.rem(c, 4) * SM, SM), SM)

    def span(c, n):
        return pl.ds(pl.multiple_of(c * n, SM), n)

    def inside(c, n):
        return pl.ds(pl.multiple_of(lax.rem(c, BLK // n) * n, SM), n)

    def f_copy(c):
        return remote(f_hbm.at[small(c)], fp.at[small(c)], f_send.at[c], f_recv.at[c], p_dev)

    def t_copy(c):
        return remote(t_hbm.at[small(c)], tq.at[c // 4, part(c)], t_send.at[c], t_recv.at[c], q_dev)

    def di_copy(c):
        return remote(si.at[small(c)], ri.at[small(c)], di_send.at[c], di_recv.at[c], p_dev)

    def dt_copy(c):
        return remote(st.at[small(c)], rt.at[small(c)], dt_send.at[c], dt_recv.at[c], q_dev)

    for c in range(NSM):
        f_copy(c).start()
        t_copy(c).start()
    w_in = pltpu.make_async_copy(w_hbm, w, in_sem.at[0])
    f_in = pltpu.make_async_copy(f_hbm, fn, in_sem.at[1])
    t_in = pltpu.make_async_copy(t_hbm, tn, in_sem.at[2])
    w_in.start()
    f_in.start()
    t_in.start()

    for copy in scalars:
        copy.wait()
    scale = scale_ref[0]
    offset = offset_ref[0]

    def pair(g, h):
        first = cap_ref[g, 0, 0, h]
        a0, a1, live = img_ref[g, 0, 0, h], img_ref[g, 0, 1, h], cnt_ref[g, 0, h]
        out = []
        for k in range(2):
            slot = jnp.abs(first - k)
            out.append((a0 + (a1 - a0) * slot, jnp.clip(live - slot, 0, 1).astype(F32)))
        return out

    pair_a, pair_b, pair_c = pair(gp, me), pair(me, gq), pair(gp, gq)

    def hit(sel, b):
        return (1 - jnp.abs(sel - b)).astype(F32)

    def norm(v):
        return lax.rsqrt(jnp.sum(v * v, axis=-1, keepdims=True) + EPS)

    def project(g, u, r):
        return (g - u * jnp.sum(g * u, axis=-1, keepdims=True)) * r

    def loop(n, body, start=0):
        lax.fori_loop(start, n, lambda i, _: (body(i), 0)[1], 0)

    def embed(f_ref, where):
        e = mm(f_ref[where, :], w[...], NN)
        r = norm(e)
        return e * r, r

    w_in.wait()
    f_in.wait()

    def embed_own(c):
        unit, r = embed(fn, rows(c))
        unit32[rows(c), :] = unit
        inv[rows(c), 0:1] = r
        iun[c // 2, half(c), :] = unit.astype(BF)

    loop(NCH, embed_own)
    t_in.wait()

    def text_own(c):
        v = tn[rows(c), :].astype(F32)
        r = norm(v)
        inv[rows(c), 2:3] = r
        tun[c // 2, half(c), :] = (v * r).astype(BF)

    loop(NCH, text_own)

    def line(b, start, n):
        return pl.ds(pl.multiple_of(b * BLK + start, SM), n)

    def tile(images, sel, texts, k, slot, live, diagonal):
        def body(r):
            s = mm(images[sel, half(r), :], texts[k], NT) * scale + offset
            if diagonal:
                on = (lax.broadcasted_iota(jnp.int32, s.shape, 0) + r * CH) == lax.broadcasted_iota(jnp.int32, s.shape, 1)
                s = jnp.where(on, -s, s)
            e = jnp.exp(s)
            g = e / (1.0 + e)
            if diagonal:
                g = jnp.where(on, -g, g)
            else:
                g = g * live
            gs[slot, half(r), :] = g.astype(BF)
            total = jnp.sum(jnp.log1p(e), axis=1, keepdims=True)
            return total

        return body

    def tile_diag(k):
        body = tile(iun, k, tun, k, k, None, True)

        def step(r):
            inv[line(k, r * CH, CH), 3:4] = body(r)

        loop(2, step)

    def tile_own(k, slot):
        sel, live = pair_b[k]
        body = tile(iun, sel, tq, k, slot, live, False)

        def step(r):
            total = body(r) * live
            for b in range(2):
                where = line(b, r * CH, CH)
                inv[where, 3:4] = inv[where, 3:4] + total * hit(sel, b)

        loop(2, step)

    def piece(b, r0, nr, k, c0, nc):
        sel, live = pair_c[k]
        keep = live * hit(sel, b)
        e = jnp.exp(mm(iup[b, r0 : r0 + nr, :], tq[k, c0 : c0 + nc, :], NT) * scale + offset)
        gs[8 + 2 * k + b, r0 : r0 + nr, c0 : c0 + nc] = (e / (1.0 + e) * keep).astype(BF)
        where = pl.ds(b * BLK + r0, nr)
        inv[where, 4:5] = inv[where, 4:5] + jnp.sum(jnp.log1p(e), axis=1, keepdims=True) * keep

    loop(2, tile_diag)

    def own_diag(c):
        b = c // 2
        din[rows(c), :] = mm(gs[b, half(c), :], tun[b], NN) * scale

    loop(NCH, own_diag)

    def arrive_image(c):
        f_copy(c).wait_recv()
        unit, r = embed(fp, small(c))
        wide[small(c), :] = unit
        inv[small(c), 1:2] = r
        inv[small(c), 4:5] = jnp.zeros((SM, 1), F32)
        iup[c // 4, part(c), :] = unit.astype(BF)

    def near(c):
        b = c // 4
        total = inv[small(c), 4:5]
        for k in range(2):
            sel, live = pair_a[k]
            keep = live * hit(sel, b)
            e = jnp.exp(mm(iup[b, part(c), :], tun[k], NT) * scale + offset)
            gs[2 + 2 * k + b, part(c), :] = (e / (1.0 + e) * keep).astype(BF)
            total = total + jnp.sum(jnp.log1p(e), axis=1, keepdims=True) * keep
        inv[small(c), 4:5] = total

    def arrive_text(c):
        t_copy(c).wait_recv()
        v = tq[c // 4, part(c), :].astype(F32)
        tq[c // 4, part(c), :] = (v * norm(v)).astype(BF)

    def arrive(c):
        arrive_image(c)
        near(c)
        arrive_text(c)

    loop(4, arrive)
    tile_own(0, 6)

    def back_text(cols, parts):
        out = None
        for slot, images, sel in parts:
            v = mm(gs[slot, :, cols], images[sel], TN)
            out = v if out is None else out + v
        return out * scale

    def back_image(b, lines, parts):
        out = None
        for slot, texts, k, sel in parts:
            g = gs[slot, lines, :]
            if sel is not None:
                g = (g.astype(F32) * hit(sel, b)).astype(BF)
            v = mm(g, texts[k], NN)
            out = v if out is None else out + v
        return out * scale

    def own_first(c):
        din[rows(c), :] = din[rows(c), :] + back_image(c // 2, half(c), ((6, tq, 0, pair_b[0][0]),))

    loop(NCH, own_first)
    piece(0, 0, 256, 0, 0, 512)
    piece(0, 256, 256, 0, 0, 512)
    loop(6, arrive, 4)
    piece(1, 0, 256, 0, 0, 512)
    piece(1, 0, 256, 1, 0, 256)
    piece(0, 0, 512, 1, 0, 256)
    loop(7, arrive, 6)
    piece(1, 256, 128, 0, 0, 512)
    piece(1, 256, 128, 1, 0, 384)
    piece(0, 0, 512, 1, 256, 128)
    piece(1, 0, 256, 1, 256, 128)
    def send_text(c, n=CH):
        k = c // (BLK // n)
        sel_b = jnp.where(k == 0, pair_b[0][0], pair_b[1][0])
        sel_c = jnp.where(k == 0, pair_c[0][0], pair_c[1][0])
        v = back_text(inside(c, n), ((6 + k, iun, sel_b), (8 + 2 * k + sel_c, iup, sel_c)))
        st[span(c, n), :] = v.astype(BF)
        for i in range(n // SM):
            dt_copy(c * (n // SM) + i).start()

    def send_image(c, n=CH, held=0):
        b = c // (BLK // n)
        g = back_image(
            b, inside(c, n), ((2 + b, tun, 0, None), (4 + b, tun, 1, None), (8 + b, tq, 0, None), (10 + b, tq, 1, None))
        )
        si[span(c, n), :] = g.astype(BF)
        for i in range(n // SM - held):
            di_copy(c * (n // SM) + i).start()
        ep[span(c, n), :] = project(g, wide[span(c, n), :], inv[span(c, n), 1:2]).astype(BF)

    loop(NSM, arrive_text, NSM - 1)
    piece(0, 0, 512, 1, 384, 128)
    loop(2, lambda c: send_image(c, SM))
    loop(NSM, arrive_image, NSM - 1)
    piece(1, 384, 128, 0, 0, 512)
    loop(2, lambda c: send_text(c, SM))
    loop(NSM, near, NSM - 1)
    piece(1, 384, 128, 1, 0, 512)
    piece(1, 0, 384, 1, 384, 128)
    loop(NCH - 1, send_image, 1)
    loop(NCH, lambda c: send_image(c, CH, 1), NCH - 1)
    loop(2, send_text, 1)

    def row_form(at_col, out):
        for i in range(8):
            v = inv[pl.ds(i * 128, 128), at_col : at_col + 1]
            out[pl.ds(i, 1), :] = jnp.transpose(jnp.broadcast_to(v, (128, 128)))[0:1, :]

    row_form(4, ls)
    l_copy = remote(ls, lr, l_sem.at[0], l_sem.at[1], p_dev)
    l_copy.start()
    tile_own(1, 7)

    def own_image(c):
        g = din[rows(c), :] + back_image(c // 2, half(c), ((7, tq, 1, pair_b[1][0]),))
        din[rows(c), :] = g
        tun[c // 2, half(c), :] = project(g, unit32[rows(c), :], inv[rows(c), 0:1]).astype(BF)

    loop(NCH, own_image)

    def head(cols, hs, by_y):
        def step(j):
            own = pl.ds(pl.multiple_of(j * 384, 128), 384)
            h = mm(fp[:, own], ep[:, cols], TN)
            h = h + mm(fn[pl.ds(0, BLK), own], tun[0, :, cols], TN) + mm(fn[pl.ds(BLK, BLK), own], tun[1, :, cols], TN)
            wide[own, cols] = h

        loop(3, step)

        def split(j):
            v = []
            for i in range(4):
                at_row = (j * 4 + i if by_y else i * 4 + j) * 2 * HR
                v.append(wide[pl.ds(pl.multiple_of(at_row, 8), 2 * HR), cols])
            for c in range(2):
                hs[c, j] = jnp.concatenate([u[c * HR : (c + 1) * HR, :] for u in v], axis=0).astype(BF)

        loop(4, split)

    lo_cols, hi_cols = pl.ds(0, LO), pl.ds(LO, HI)
    head(lo_cols, hs_lo, False)
    c_lo = remote(hs_lo.at[1 - core], rc_lo, c_sem.at[0], c_sem.at[1], c_dev)
    c_lo.start()
    head(hi_cols, hs_hi, True)
    c_hi = remote(hs_hi.at[1 - core], rc_hi, c_sem.at[2], c_sem.at[3], c_dev)
    c_hi.start()

    def add_core(rc, hs):
        def step(j):
            rc[j] = (rc[j].astype(F32) + hs[core, j].astype(F32)).astype(BF)

        loop(4, step)

    c_lo.wait()
    add_core(rc_lo, hs_lo)
    xc = [remote(rc_lo.at[xs[d]], rx.at[d], x_send.at[d], x_recv.at[d], x_devs[d]) for d in range(3)]
    for copy in xc:
        copy.start()
    loop(NCH, send_text, 2)
    c_hi.wait()
    add_core(rc_hi, hs_hi)
    yc = [
        remote(rc_hi.at[ys[d]], ry.at[d], y_send.at[d], y_recv.at[d], y_devs[d]) for d in range(3)
    ]
    for copy in yc:
        copy.start()

    def own_text(c):
        b = c // 2
        sel = jnp.where(b == 0, pair_a[0][0], pair_a[1][0])
        v = mm(gs[b, :, half(c)], iun[b], TN) + mm(gs[2 + 2 * b + sel, :, half(c)], iup[sel], TN)
        wide[rows(c), :] = v * scale

    loop(NCH, own_text)

    def finish(c, n=CH):
        where = span(c, n)
        b = c // (BLK // n)
        for i in range(n // SM):
            di_copy(c * (n // SM) + i).wait_recv()
        g = din[where, :] + ri[where, :].astype(F32)
        eg = project(g, unit32[where, :], inv[where, 0:1]).astype(BF)
        iup[b, inside(c, n), :] = mm(eg, w[...], NT).astype(BF)
        for i in range(n // SM):
            dt_copy(c * (n // SM) + i).wait_recv()
        u = tn[where, :].astype(F32) * inv[where, 2:3]
        gt = wide[where, :] + rt[where, :].astype(F32)
        iun[b, inside(c, n), :] = project(gt, u, inv[where, 2:3]).astype(BF)

    loop(2, finish)

    def fold(rc, mine, recv, out):
        v = rc[mine].astype(F32)
        for d in range(3):
            v = v + recv[d].astype(F32)
        zero = jnp.zeros((HP - HR, v.shape[1]), F32)
        for i in range(4):
            out[i] = jnp.concatenate([v[i * HR : (i + 1) * HR, :], zero], axis=0).astype(BF)

    for copy in xc:
        copy.wait()
    fold(rc_lo, x, rx, ba)
    second = [remote(ba.at[ys[d]], r2a.at[d], y2_send.at[d], y2_recv.at[d], y_devs[d]) for d in range(3)]
    for copy in second:
        copy.start()
    for copy in yc:
        copy.wait()
    fold(rc_hi, y, ry, bb)
    third = [remote(bb.at[xs[d]], r2b.at[d], x2_send.at[d], x2_recv.at[d], x_devs[d]) for d in range(3)]
    for copy in third:
        copy.start()
    loop(3, finish, 2)
    for copy in second + third:
        copy.wait()
    lo = ba[y].astype(F32)
    hi = bb[x].astype(F32)
    for d in range(3):
        lo = lo + r2a[d].astype(F32)
        hi = hi + r2b[d].astype(F32)
    zs[0, :, pl.ds(0, LO)] = lo.astype(BF)
    zs[0, :, pl.ds(LO, HI)] = hi.astype(BF)
    z0 = remote(zs.at[0], zr.at[0], z_send.at[0], z_recv.at[0], p_dev)
    z0.start()
    di_copy(NSM - 1).start()
    z0.wait()
    zs[1] = (zs[0].astype(F32) + zr[0].astype(F32)).astype(BF)
    z1 = remote(zs.at[1], zr.at[1], z_send.at[1], z_recv.at[1], q_dev)
    z1.start()
    loop(NSM - 1, lambda c: finish(c, SM), NSM - 2)
    loop(NSM, lambda c: finish(c, SM), NSM - 1)
    l_copy.wait()
    row_form(3, ls)
    loss_out[...] = (ls[...] + lr[...]) * (1.0 / BLK)
    z1.wait()
    head_out[...] = (zs[1].astype(F32) + zr[1].astype(F32))[0:HR, :]

    def sent(c):
        f_copy(c).wait_send()
        t_copy(c).wait_send()
        di_copy(c).wait_send()
        dt_copy(c).wait_send()

    loop(NSM, sent)


def emit(loss, pooled, text, grad, loss_out, pooled_out, text_out, grad_out, sem):
    copies = [pltpu.make_async_copy(grad, grad_out, sem.at[8])]
    for i in range(4):
        where = pl.ds(i % 2 * CH, CH)
        copies.append(pltpu.make_async_copy(pooled.at[i // 2, where], pooled_out.at[i // 2, where], sem.at[i]))
        copies.append(pltpu.make_async_copy(text.at[i // 2, where], text_out.at[i // 2, where], sem.at[4 + i]))
    for copy in copies:
        copy.start()
    for i in range(8):
        loss_out[pl.ds(i * 128, 128)] = loss[i, :]
    for copy in copies:
        copy.wait()


def per_device(features, captions, head, scaling, offset, img, cap, cnt):
    hbm = pl.BlockSpec(memory_space=pl.ANY)
    smem = pl.BlockSpec(memory_space=pltpu.SMEM)
    vmem = pl.BlockSpec(memory_space=pltpu.VMEM)
    big = pltpu.VMEM((ROWS, D), BF)
    blocks = pltpu.VMEM((2, BLK, D), BF)
    dma = pltpu.SemaphoreType.DMA
    loss, pooled, text, grad = pl.pallas_call(
        kernel,
        out_shape=(pltpu.VMEM((8, 128), F32), blocks, blocks, pltpu.VMEM((HR, D), F32)),
        in_specs=[hbm] * 3 + [smem] * 2 + [hbm] * 3,
        out_specs=(vmem, vmem, vmem, vmem),
        scratch_shapes=[
            pltpu.SMEM((4, 1, 2, 4), jnp.int32), pltpu.SMEM((4, 1, 2, 4), jnp.int32), pltpu.SMEM((4, 1, 4), jnp.int32),
            big, big, big, blocks, blocks, pltpu.VMEM((D, D), BF),
            pltpu.VMEM((ROWS, D), F32), pltpu.VMEM((ROWS, D), F32), pltpu.VMEM((D, D), F32),
            big, big, big, big, pltpu.VMEM((12, BLK, BLK), BF), big,
            pltpu.VMEM((2, 4, 4 * HR, LO), BF), pltpu.VMEM((2, 4, 4 * HR, HI), BF),
            pltpu.VMEM((4, 4 * HR, LO), BF), pltpu.VMEM((4, 4 * HR, HI), BF),
            pltpu.VMEM((3, 4 * HR, LO), BF), pltpu.VMEM((3, 4 * HR, HI), BF),
            pltpu.VMEM((4, HP, LO), BF), pltpu.VMEM((4, HP, HI), BF),
            pltpu.VMEM((3, HP, LO), BF), pltpu.VMEM((3, HP, HI), BF),
            pltpu.VMEM((2, HP, D), BF), pltpu.VMEM((2, HP, D), BF),
            pltpu.VMEM((ROWS, 5), F32),
            pltpu.VMEM((8, 128), F32), pltpu.VMEM((8, 128), F32),
            dma((NSM,)), dma((NSM,)), dma((NSM,)), dma((NSM,)), dma((NSM,)), dma((NSM,)), dma((NSM,)), dma((NSM,)),
            dma((2,)), dma((4,)), dma((3,)), dma((3,)), dma((3,)), dma((3,)), dma((3,)), dma((3,)), dma((3,)), dma((3,)),
            dma((2,)), dma((2,)), dma((6,)),
        ],
        compiler_params=pltpu.CompilerParams(
            collective_id=0, has_side_effects=True, vmem_limit_bytes=57 << 20
        ),
        cost_estimate=pl.CostEstimate(flops=34_000_000_000, bytes_accessed=20_000_000, transcendentals=6_000_000),
    )(features, captions, head, scaling, offset, jnp.swapaxes(img, 2, 3), jnp.swapaxes(cap, 2, 3), cnt)
    loss, pooled, text, grad = pl.pallas_call(
        emit,
        out_shape=(
            jax.ShapeDtypeStruct((ROWS,), F32),
            jax.ShapeDtypeStruct((2, BLK, D), BF),
            jax.ShapeDtypeStruct((2, BLK, D), BF),
            jax.ShapeDtypeStruct((HR, D), F32),
        ),
        in_specs=[vmem, hbm, hbm, hbm],
        out_specs=(vmem, hbm, hbm, hbm),
        scratch_shapes=[dma((9,))],
        compiler_params=pltpu.CompilerParams(vmem_limit_bytes=4 << 20),
    )(*(pltpu.with_memory_space_constraint(v, pltpu.VMEM) for v in (loss, pooled, text, grad)))
    return loss, pooled.reshape(ROWS, D), text.reshape(ROWS, D), grad


def solution(mesh):
    return jax.shard_map(
        per_device,
        mesh=mesh,
        in_specs=(
            P(("grp", "inner"), None),
            P(("grp", "inner"), None),
            P(),
            P(),
            P(),
            P(None, "inner", None, None),
            P(None, "inner", None, None),
            P(None, "inner", None),
        ),
        out_specs=(
            P(("grp", "inner")),
            P(("grp", "inner"), None),
            P(("grp", "inner"), None),
            P("inner", None),
        ),
        check_vma=False,
    )
```

```python
import functools

import jax
import jax.numpy as jnp
from jax import lax
from jax.experimental import pallas as pl
from jax.experimental.pallas import tpu as pltpu
from jax.sharding import PartitionSpec as P

MESH = pl.DeviceIdType.MESH
BLK = 512
D = 1152
ROWS = 1024
CH = 256
NCH = ROWS // CH
SM = 128
NSM = ROWS // SM
EPS = 1e-06
HR = 36
HP = 48
LO = 640
HI = D - LO
BF = jnp.bfloat16
F32 = jnp.float32

NN = (((1,), (0,)), ((), ()))
NT = (((1,), (1,)), ((), ()))
TN = (((0,), (0,)), ((), ()))


def mm(a, b, dims):
    return lax.dot_general(a, b, dims, preferred_element_type=F32)


def kernel(
    f_hbm, t_hbm, w_hbm, scale_ref, offset_ref, img_hbm, cap_hbm, cnt_hbm,
    loss_out, iup, iun, head_out,
    img_ref, cap_ref, cnt_ref,
    fn, fp, tn, tun, tq, w, unit32, din, wide, si, st, ri, rt, gs, ep,
    hs_lo, hs_hi, rc_lo, rc_hi, rx, ry, ba, bb, r2a, r2b, zs, zr, zt, zu, pre, inv, ls, lr,
    f_send, f_recv, t_send, t_recv, di_send, di_recv, dt_send, dt_recv,
    l_sem, c_sem, x_send, x_recv, y_send, y_recv, x2_send, x2_recv, y2_send, y2_recv,
    z_send, z_recv, in_sem,
):
    me = lax.axis_index("grp")
    inner = lax.axis_index("inner")
    odd = lax.rem(me, 2)
    gp = lax.rem(me + 3 + 2 * odd, 4)
    gq = lax.rem(me + 1 + 2 * odd, 4)
    core = lax.rem(inner, 2)
    x = lax.rem(inner // 2, 4)
    y = inner // 8

    def at(yy, xx, cc):
        return (yy * 4 + xx) * 2 + cc

    p_dev, q_dev = (gp, inner), (gq, inner)
    c_dev = (me, at(y, x, 1 - core))
    xs = [lax.rem(x + d, 4) for d in (1, 2, 3)]
    ys = [lax.rem(y + d, 4) for d in (1, 2, 3)]
    x_devs = [(me, at(y, v, core)) for v in xs]
    y_devs = [(me, at(v, x, core)) for v in ys]

    def remote(src, dst, send, recv, dev):
        return pltpu.make_async_remote_copy(
            src_ref=src, dst_ref=dst, send_sem=send, recv_sem=recv, device_id=dev, device_id_type=MESH
        )

    scalars = [
        pltpu.make_async_copy(src, dst, in_sem.at[3 + i])
        for i, (src, dst) in enumerate(((img_hbm, img_ref), (cap_hbm, cap_ref), (cnt_hbm, cnt_ref)))
    ]
    for copy in scalars:
        copy.start()
    barrier = pltpu.get_barrier_semaphore()
    peers = [p_dev, q_dev, c_dev] + x_devs + y_devs
    for dev in peers:
        pl.semaphore_signal(barrier, inc=1, device_id=dev, device_id_type=MESH)
    pl.semaphore_wait(barrier, len(peers))

    def rows(c):
        return pl.ds(pl.multiple_of(c * CH, CH), CH)

    def half(c):
        return pl.ds(pl.multiple_of(lax.rem(c, 2) * CH, CH), CH)

    def small(c):
        return pl.ds(pl.multiple_of(c * SM, SM), SM)

    def part(c):
        return pl.ds(pl.multiple_of(lax.rem(c, 4) * SM, SM), SM)

    def span(c, n):
        return pl.ds(pl.multiple_of(c * n, SM), n)

    def inside(c, n):
        return pl.ds(pl.multiple_of(lax.rem(c, BLK // n) * n, SM), n)

    def f_copy(c):
        return remote(f_hbm.at[small(c)], fp.at[small(c)], f_send.at[c], f_recv.at[c], p_dev)

    def t_copy(c):
        return remote(t_hbm.at[small(c)], tq.at[c // 4, part(c)], t_send.at[c], t_recv.at[c], q_dev)

    def di_copy(c):
        return remote(si.at[small(c)], ri.at[small(c)], di_send.at[c], di_recv.at[c], p_dev)

    def dt_copy(c):
        return remote(st.at[small(c)], rt.at[small(c)], dt_send.at[c], dt_recv.at[c], q_dev)

    for c in range(NSM):
        f_copy(c).start()
        t_copy(c).start()
    w_in = pltpu.make_async_copy(w_hbm, w, in_sem.at[0])
    f_in = pltpu.make_async_copy(f_hbm, fn, in_sem.at[1])
    t_in = pltpu.make_async_copy(t_hbm, tn, in_sem.at[2])
    w_in.start()
    f_in.start()
    t_in.start()

    for copy in scalars:
        copy.wait()
    scale = scale_ref[0]
    offset = offset_ref[0]

    def pair(g, h):
        first = cap_ref[g, 0, 0, h]
        a0, a1, live = img_ref[g, 0, 0, h], img_ref[g, 0, 1, h], cnt_ref[g, 0, h]
        out = []
        for k in range(2):
            slot = jnp.abs(first - k)
            out.append((a0 + (a1 - a0) * slot, jnp.clip(live - slot, 0, 1).astype(F32)))
        return out

    pair_a, pair_b, pair_c = pair(gp, me), pair(me, gq), pair(gp, gq)

    def hit(sel, b):
        return (1 - jnp.abs(sel - b)).astype(F32)

    def norm(v):
        return lax.rsqrt(jnp.sum(v * v, axis=-1, keepdims=True) + EPS)

    def project(g, u, r):
        return (g - u * jnp.sum(g * u, axis=-1, keepdims=True)) * r

    def loop(n, body, start=0):
        lax.fori_loop(start, n, lambda i, _: (body(i), 0)[1], 0)

    def embed(f_ref, where):
        e = mm(f_ref[where, :], w[...], NN)
        r = norm(e)
        return e * r, r

    w_in.wait()
    f_in.wait()

    def embed_own(c):
        unit, r = embed(fn, rows(c))
        unit32[rows(c), :] = unit
        inv[rows(c), 0:1] = r
        iun[c // 2, half(c), :] = unit.astype(BF)

    loop(NCH, embed_own)
    t_in.wait()

    def text_own(c):
        v = tn[rows(c), :].astype(F32)
        r = norm(v)
        inv[rows(c), 2:3] = r
        tun[c // 2, half(c), :] = (v * r).astype(BF)

    loop(NCH, text_own)

    def line(b, start, n):
        return pl.ds(pl.multiple_of(b * BLK + start, SM), n)

    def tile(images, sel, texts, k, slot, live, diagonal):
        def body(r):
            s = mm(images[sel, half(r), :], texts[k], NT) * scale + offset
            if diagonal:
                on = (lax.broadcasted_iota(jnp.int32, s.shape, 0) + r * CH) == lax.broadcasted_iota(jnp.int32, s.shape, 1)
                s = jnp.where(on, -s, s)
            e = jnp.exp(s)
            g = e / (1.0 + e)
            if diagonal:
                g = jnp.where(on, -g, g)
            else:
                g = g * live
            gs[slot, half(r), :] = g.astype(BF)
            total = jnp.sum(jnp.log1p(e), axis=1, keepdims=True)
            return total

        return body

    def tile_diag(k):
        body = tile(iun, k, tun, k, k, None, True)

        def step(r):
            inv[line(k, r * CH, CH), 3:4] = body(r)

        loop(2, step)

    def tile_own(k, slot):
        sel, live = pair_b[k]
        body = tile(iun, sel, tq, k, slot, live, False)

        def step(r):
            total = body(r) * live
            for b in range(2):
                where = line(b, r * CH, CH)
                inv[where, 3:4] = inv[where, 3:4] + total * hit(sel, b)

        loop(2, step)

    def piece(b, r0, nr, k, c0, nc):
        sel, live = pair_c[k]
        keep = live * hit(sel, b)
        e = jnp.exp(mm(iup[b, r0 : r0 + nr, :], tq[k, c0 : c0 + nc, :], NT) * scale + offset)
        gs[8 + 2 * k + b, r0 : r0 + nr, c0 : c0 + nc] = (e / (1.0 + e) * keep).astype(BF)
        where = pl.ds(b * BLK + r0, nr)
        inv[where, 4:5] = inv[where, 4:5] + jnp.sum(jnp.log1p(e), axis=1, keepdims=True) * keep

    loop(2, tile_diag)

    def own_diag(c):
        b = c // 2
        din[rows(c), :] = mm(gs[b, half(c), :], tun[b], NN) * scale

    loop(NCH, own_diag)

    def arrive_image(c):
        f_copy(c).wait_recv()
        unit, r = embed(fp, small(c))
        wide[small(c), :] = unit
        inv[small(c), 1:2] = r
        inv[small(c), 4:5] = jnp.zeros((SM, 1), F32)
        iup[c // 4, part(c), :] = unit.astype(BF)

    def near(c):
        b = c // 4
        total = inv[small(c), 4:5]
        for k in range(2):
            sel, live = pair_a[k]
            keep = live * hit(sel, b)
            e = jnp.exp(mm(iup[b, part(c), :], tun[k], NT) * scale + offset)
            gs[2 + 2 * k + b, part(c), :] = (e / (1.0 + e) * keep).astype(BF)
            total = total + jnp.sum(jnp.log1p(e), axis=1, keepdims=True) * keep
        inv[small(c), 4:5] = total

    def arrive_text(c):
        t_copy(c).wait_recv()
        v = tq[c // 4, part(c), :].astype(F32)
        tq[c // 4, part(c), :] = (v * norm(v)).astype(BF)

    def arrive(c):
        arrive_image(c)
        near(c)
        arrive_text(c)

    loop(4, arrive)
    tile_own(0, 6)

    def back_text(cols, parts):
        out = None
        for slot, images, sel in parts:
            v = mm(gs[slot, :, cols], images[sel], TN)
            out = v if out is None else out + v
        return out * scale

    def back_image(b, lines, parts):
        out = None
        for slot, texts, k, sel in parts:
            g = gs[slot, lines, :]
            if sel is not None:
                g = (g.astype(F32) * hit(sel, b)).astype(BF)
            v = mm(g, texts[k], NN)
            out = v if out is None else out + v
        return out * scale

    def own_first(c):
        din[rows(c), :] = din[rows(c), :] + back_image(c // 2, half(c), ((6, tq, 0, pair_b[0][0]),))

    loop(NCH, own_first)
    piece(0, 0, 256, 0, 0, 512)
    piece(0, 256, 256, 0, 0, 512)
    loop(6, arrive, 4)
    piece(1, 0, 256, 0, 0, 512)
    piece(1, 0, 256, 1, 0, 256)
    piece(0, 0, 512, 1, 0, 256)
    loop(7, arrive, 6)
    piece(1, 256, 128, 0, 0, 512)
    piece(1, 256, 128, 1, 0, 384)
    piece(0, 0, 512, 1, 256, 128)
    piece(1, 0, 256, 1, 256, 128)
    def send_text(c, n=CH):
        k = c // (BLK // n)
        sel_b = jnp.where(k == 0, pair_b[0][0], pair_b[1][0])
        sel_c = jnp.where(k == 0, pair_c[0][0], pair_c[1][0])
        v = back_text(inside(c, n), ((6 + k, iun, sel_b), (8 + 2 * k + sel_c, iup, sel_c)))
        st[span(c, n), :] = v.astype(BF)
        for i in range(n // SM):
            dt_copy(c * (n // SM) + i).start()

    def send_image(c, n=CH, held=0):
        b = c // (BLK // n)
        g = back_image(
            b, inside(c, n), ((2 + b, tun, 0, None), (4 + b, tun, 1, None), (8 + b, tq, 0, None), (10 + b, tq, 1, None))
        )
        si[span(c, n), :] = g.astype(BF)
        for i in range(n // SM - held):
            di_copy(c * (n // SM) + i).start()
        ep[span(c, n), :] = project(g, wide[span(c, n), :], inv[span(c, n), 1:2]).astype(BF)

    start = back_image(0, pl.ds(0, SM), ((2, tun, 0, None), (4, tun, 1, None), (8, tq, 0, None)))
    pre[0] = start + mm(gs[10, 0:SM, 0:384], tq[1, 0:384, :], NN) * scale
    pre[1] = back_text(pl.ds(0, SM), ((6, iun, pair_b[0][0]),))
    loop(NSM, arrive_text, NSM - 1)
    piece(0, 0, 512, 1, 384, 128)
    first_image = pre[0] + mm(gs[10, 0:SM, 384:512], tq[1, 384:512, :], NN) * scale
    si[0:SM, :] = first_image.astype(BF)
    loop(1, lambda c: di_copy(c).start())
    pre[0] = first_image
    loop(NSM, arrive_image, NSM - 1)
    piece(1, 384, 128, 0, 0, 512)
    first_text = pre[1] + back_text(pl.ds(0, SM), ((8 + pair_c[0][0], iup, pair_c[0][0]),))
    st[0:SM, :] = first_text.astype(BF)
    loop(1, lambda c: dt_copy(c).start())
    ep[0:SM, :] = project(pre[0], wide[0:SM, :], inv[0:SM, 1:2]).astype(BF)
    loop(2, lambda c: send_image(c, SM), 1)
    loop(2, lambda c: send_text(c, SM), 1)
    loop(NSM, near, NSM - 1)
    piece(1, 384, 128, 1, 0, 512)
    piece(1, 0, 384, 1, 384, 128)
    loop(NCH - 1, send_image, 1)
    loop(NCH, lambda c: send_image(c, CH, 1), NCH - 1)
    loop(2, send_text, 1)

    def row_form(at_col, out):
        for i in range(8):
            v = inv[pl.ds(i * 128, 128), at_col : at_col + 1]
            out[pl.ds(i, 1), :] = jnp.transpose(jnp.broadcast_to(v, (128, 128)))[0:1, :]

    row_form(4, ls)
    l_copy = remote(ls, lr, l_sem.at[0], l_sem.at[1], p_dev)
    l_copy.start()
    tile_own(1, 7)

    def own_image(c):
        g = din[rows(c), :] + back_image(c // 2, half(c), ((7, tq, 1, pair_b[1][0]),))
        din[rows(c), :] = g
        tun[c // 2, half(c), :] = project(g, unit32[rows(c), :], inv[rows(c), 0:1]).astype(BF)

    loop(NCH, own_image)

    def head(cols, hs, by_y):
        def step(j):
            own = pl.ds(pl.multiple_of(j * 384, 128), 384)
            h = mm(fp[:, own], ep[:, cols], TN)
            h = h + mm(fn[pl.ds(0, BLK), own], tun[0, :, cols], TN) + mm(fn[pl.ds(BLK, BLK), own], tun[1, :, cols], TN)
            wide[own, cols] = h

        loop(3, step)

        def split(j):
            v = []
            for i in range(4):
                at_row = (j * 4 + i if by_y else i * 4 + j) * 2 * HR
                v.append(wide[pl.ds(pl.multiple_of(at_row, 8), 2 * HR), cols])
            for c in range(2):
                hs[c, j] = jnp.concatenate([u[c * HR : (c + 1) * HR, :] for u in v], axis=0).astype(BF)

        loop(4, split)

    lo_cols, hi_cols = pl.ds(0, LO), pl.ds(LO, HI)
    head(lo_cols, hs_lo, False)
    c_lo = remote(hs_lo.at[1 - core], rc_lo, c_sem.at[0], c_sem.at[1], c_dev)
    c_lo.start()
    head(hi_cols, hs_hi, True)
    c_hi = remote(hs_hi.at[1 - core], rc_hi, c_sem.at[2], c_sem.at[3], c_dev)
    c_hi.start()

    def add_core(rc, hs):
        def step(j):
            rc[j] = (rc[j].astype(F32) + hs[core, j].astype(F32)).astype(BF)

        loop(4, step)

    c_lo.wait()
    add_core(rc_lo, hs_lo)
    xc = [remote(rc_lo.at[xs[d]], rx.at[d], x_send.at[d], x_recv.at[d], x_devs[d]) for d in range(3)]
    for copy in xc:
        copy.start()
    loop(NCH, send_text, 2)
    c_hi.wait()
    add_core(rc_hi, hs_hi)
    yc = [
        remote(rc_hi.at[ys[d]], ry.at[d], y_send.at[d], y_recv.at[d], y_devs[d]) for d in range(3)
    ]
    for copy in yc:
        copy.start()

    def own_text(c):
        b = c // 2
        sel = jnp.where(b == 0, pair_a[0][0], pair_a[1][0])
        v = mm(gs[b, :, half(c)], iun[b], TN) + mm(gs[2 + 2 * b + sel, :, half(c)], iup[sel], TN)
        wide[rows(c), :] = v * scale

    loop(NCH, own_text)

    def finish(c, n=CH):
        where = span(c, n)
        b = c // (BLK // n)
        for i in range(n // SM):
            di_copy(c * (n // SM) + i).wait_recv()
        g = din[where, :] + ri[where, :].astype(F32)
        eg = project(g, unit32[where, :], inv[where, 0:1]).astype(BF)
        iup[b, inside(c, n), :] = mm(eg, w[...], NT).astype(BF)
        for i in range(n // SM):
            dt_copy(c * (n // SM) + i).wait_recv()
        u = tn[where, :].astype(F32) * inv[where, 2:3]
        gt = wide[where, :] + rt[where, :].astype(F32)
        iun[b, inside(c, n), :] = project(gt, u, inv[where, 2:3]).astype(BF)

    loop(2, finish)

    def fold(rc, mine, recv, out):
        v = rc[mine].astype(F32)
        for d in range(3):
            v = v + recv[d].astype(F32)
        zero = jnp.zeros((HP - HR, v.shape[1]), F32)
        for i in range(4):
            out[i] = jnp.concatenate([v[i * HR : (i + 1) * HR, :], zero], axis=0).astype(BF)

    for copy in xc:
        copy.wait()
    fold(rc_lo, x, rx, ba)
    second = [remote(ba.at[ys[d]], r2a.at[d], y2_send.at[d], y2_recv.at[d], y_devs[d]) for d in range(3)]
    for copy in second:
        copy.start()
    for copy in yc:
        copy.wait()
    fold(rc_hi, y, ry, bb)
    third = [remote(bb.at[xs[d]], r2b.at[d], x2_send.at[d], x2_recv.at[d], x_devs[d]) for d in range(3)]
    for copy in third:
        copy.start()
    loop(3, finish, 2)
    for copy in second + third:
        copy.wait()
    lo = ba[y].astype(F32)
    hi = bb[x].astype(F32)
    for d in range(3):
        lo = lo + r2a[d].astype(F32)
        hi = hi + r2b[d].astype(F32)
    v = jnp.concatenate([lo, hi], axis=1)
    last = [v[32:HR, i * 384 : (i + 1) * 384] for i in range(3)] + [jnp.zeros((4, 384), F32)]
    zs[0] = v[0:32, :].astype(BF)
    zt[0] = jnp.concatenate(last, axis=0).astype(BF)

    def z_copies(step, dev):
        pairs = ((zs, zr), (zt, zu))
        return [
            remote(a.at[step], b.at[step], z_send.at[2 * step + i], z_recv.at[2 * step + i], dev)
            for i, (a, b) in enumerate(pairs)
        ]

    z0 = z_copies(0, p_dev)
    for copy in z0:
        copy.start()
    di_copy(NSM - 1).start()
    for copy in z0:
        copy.wait()
    zs[1] = (zs[0].astype(F32) + zr[0].astype(F32)).astype(BF)
    zt[1] = (zt[0].astype(F32) + zu[0].astype(F32)).astype(BF)
    z1 = z_copies(1, q_dev)
    for copy in z1:
        copy.start()
    loop(NSM - 1, lambda c: finish(c, SM), NSM - 2)
    loop(NSM, lambda c: finish(c, SM), NSM - 1)
    l_copy.wait()
    row_form(3, ls)
    loss_out[...] = (ls[...] + lr[...]) * (1.0 / BLK)
    for copy in z1:
        copy.wait()
    head_out[0:32, :] = zs[1].astype(F32) + zr[1].astype(F32)
    last = zt[1].astype(F32) + zu[1].astype(F32)
    for i in range(3):
        head_out[32:HR, i * 384 : (i + 1) * 384] = last[4 * i : 4 * i + 4, :]

    def sent(c):
        f_copy(c).wait_send()
        t_copy(c).wait_send()
        di_copy(c).wait_send()
        dt_copy(c).wait_send()

    loop(NSM, sent)


def emit(loss, pooled, text, grad, loss_out, pooled_out, text_out, grad_out, line, sem):
    copies = [pltpu.make_async_copy(grad, grad_out, sem.at[8])]
    for i in range(4):
        where = pl.ds(i % 2 * CH, CH)
        copies.append(pltpu.make_async_copy(pooled.at[i // 2, where], pooled_out.at[i // 2, where], sem.at[i]))
        copies.append(pltpu.make_async_copy(text.at[i // 2, where], text_out.at[i // 2, where], sem.at[4 + i]))
    for copy in copies:
        copy.start()
    for i in range(8):
        line[pl.ds(i * 128, 128)] = loss[i, :]
    copies.append(pltpu.make_async_copy(line, loss_out, sem.at[9]))
    copies[-1].start()
    for copy in copies:
        copy.wait()


def per_device(features, captions, head, scaling, offset, img, cap, cnt):
    hbm = pl.BlockSpec(memory_space=pl.ANY)
    smem = pl.BlockSpec(memory_space=pltpu.SMEM)
    vmem = pl.BlockSpec(memory_space=pltpu.VMEM)
    big = pltpu.VMEM((ROWS, D), BF)
    blocks = pltpu.VMEM((2, BLK, D), BF)
    dma = pltpu.SemaphoreType.DMA
    loss, pooled, text, grad = pl.pallas_call(
        kernel,
        out_shape=(pltpu.VMEM((8, 128), F32), blocks, blocks, pltpu.VMEM((HR, D), F32)),
        in_specs=[hbm] * 3 + [smem] * 2 + [hbm] * 3,
        out_specs=(vmem, vmem, vmem, vmem),
        scratch_shapes=[
            pltpu.SMEM((4, 1, 2, 4), jnp.int32), pltpu.SMEM((4, 1, 2, 4), jnp.int32), pltpu.SMEM((4, 1, 4), jnp.int32),
            big, big, big, blocks, blocks, pltpu.VMEM((D, D), BF),
            pltpu.VMEM((ROWS, D), F32), pltpu.VMEM((ROWS, D), F32), pltpu.VMEM((D, D), F32),
            big, big, big, big, pltpu.VMEM((12, BLK, BLK), BF), big,
            pltpu.VMEM((2, 4, 4 * HR, LO), BF), pltpu.VMEM((2, 4, 4 * HR, HI), BF),
            pltpu.VMEM((4, 4 * HR, LO), BF), pltpu.VMEM((4, 4 * HR, HI), BF),
            pltpu.VMEM((3, 4 * HR, LO), BF), pltpu.VMEM((3, 4 * HR, HI), BF),
            pltpu.VMEM((4, HP, LO), BF), pltpu.VMEM((4, HP, HI), BF),
            pltpu.VMEM((3, HP, LO), BF), pltpu.VMEM((3, HP, HI), BF),
            pltpu.VMEM((2, 32, D), BF), pltpu.VMEM((2, 32, D), BF), pltpu.VMEM((2, 16, 384), BF), pltpu.VMEM((2, 16, 384), BF),
            pltpu.VMEM((2, SM, D), F32),
            pltpu.VMEM((ROWS, 5), F32),
            pltpu.VMEM((8, 128), F32), pltpu.VMEM((8, 128), F32),
            dma((NSM,)), dma((NSM,)), dma((NSM,)), dma((NSM,)), dma((NSM,)), dma((NSM,)), dma((NSM,)), dma((NSM,)),
            dma((2,)), dma((4,)), dma((3,)), dma((3,)), dma((3,)), dma((3,)), dma((3,)), dma((3,)), dma((3,)), dma((3,)),
            dma((4,)), dma((4,)), dma((6,)),
        ],
        compiler_params=pltpu.CompilerParams(
            collective_id=0, has_side_effects=True, vmem_limit_bytes=57 << 20
        ),
        cost_estimate=pl.CostEstimate(flops=34_000_000_000, bytes_accessed=20_000_000, transcendentals=6_000_000),
    )(features, captions, head, scaling, offset, jnp.swapaxes(img, 2, 3), jnp.swapaxes(cap, 2, 3), cnt)
    loss, pooled, text, grad = pl.pallas_call(
        emit,
        out_shape=(
            jax.ShapeDtypeStruct((ROWS,), F32),
            jax.ShapeDtypeStruct((2, BLK, D), BF),
            jax.ShapeDtypeStruct((2, BLK, D), BF),
            jax.ShapeDtypeStruct((HR, D), F32),
        ),
        in_specs=[vmem, hbm, hbm, hbm],
        out_specs=(hbm, hbm, hbm, hbm),
        scratch_shapes=[pltpu.VMEM((ROWS,), F32), dma((10,))],
        compiler_params=pltpu.CompilerParams(vmem_limit_bytes=4 << 20),
    )(*(pltpu.with_memory_space_constraint(v, pltpu.VMEM) for v in (loss, pooled, text, grad)))
    return loss, pooled.reshape(ROWS, D), text.reshape(ROWS, D), grad


def solution(mesh):
    return jax.shard_map(
        per_device,
        mesh=mesh,
        in_specs=(
            P(("grp", "inner"), None),
            P(("grp", "inner"), None),
            P(),
            P(),
            P(),
            P(None, "inner", None, None),
            P(None, "inner", None, None),
            P(None, "inner", None),
        ),
        out_specs=(
            P(("grp", "inner")),
            P(("grp", "inner"), None),
            P(("grp", "inner"), None),
            P("inner", None),
        ),
        check_vma=False,
    )
```

```python
import functools

import jax
import jax.numpy as jnp
from jax import lax
from jax.experimental import pallas as pl
from jax.experimental.pallas import tpu as pltpu
from jax.sharding import PartitionSpec as P

MESH = pl.DeviceIdType.MESH
BLK = 512
D = 1152
ROWS = 1024
CH = 256
NCH = ROWS // CH
SM = 128
NSM = ROWS // SM
EPS = 1e-06
HR = 36
HP = 48
LO = 640
HI = D - LO
BF = jnp.bfloat16
F32 = jnp.float32

NN = (((1,), (0,)), ((), ()))
NT = (((1,), (1,)), ((), ()))
TN = (((0,), (0,)), ((), ()))


def mm(a, b, dims):
    return lax.dot_general(a, b, dims, preferred_element_type=F32)


def kernel(
    f_hbm, t_hbm, w_hbm, scale_ref, offset_ref, img_hbm, cap_hbm, cnt_hbm,
    loss_out, iup, iun, head_out,
    img_ref, cap_ref, cnt_ref,
    fn, fp, tn, tun, tq, w, unit32, din, wide, si, st, ri, rt, gs, ep,
    hs_lo, hs_hi, rc_lo, rc_hi, rx, ry, ba, bb, r2a, r2b, zs, zr, zt, zu, pre, inv, ls, lr,
    f_send, f_recv, t_send, t_recv, di_send, di_recv, dt_send, dt_recv,
    l_sem, c_sem, x_send, x_recv, y_send, y_recv, x2_send, x2_recv, y2_send, y2_recv,
    z_send, z_recv, in_sem,
):
    me = lax.axis_index("grp")
    inner = lax.axis_index("inner")
    odd = lax.rem(me, 2)
    gp = lax.rem(me + 3 + 2 * odd, 4)
    gq = lax.rem(me + 1 + 2 * odd, 4)
    core = lax.rem(inner, 2)
    x = lax.rem(inner // 2, 4)
    y = inner // 8

    def at(yy, xx, cc):
        return (yy * 4 + xx) * 2 + cc

    p_dev, q_dev = (gp, inner), (gq, inner)
    c_dev = (me, at(y, x, 1 - core))
    xs = [lax.rem(x + d, 4) for d in (1, 2, 3)]
    ys = [lax.rem(y + d, 4) for d in (1, 2, 3)]
    x_devs = [(me, at(y, v, core)) for v in xs]
    y_devs = [(me, at(v, x, core)) for v in ys]

    def remote(src, dst, send, recv, dev):
        return pltpu.make_async_remote_copy(
            src_ref=src, dst_ref=dst, send_sem=send, recv_sem=recv, device_id=dev, device_id_type=MESH
        )

    scalars = [
        pltpu.make_async_copy(src, dst, in_sem.at[3 + i])
        for i, (src, dst) in enumerate(((img_hbm, img_ref), (cap_hbm, cap_ref), (cnt_hbm, cnt_ref)))
    ]
    for copy in scalars:
        copy.start()
    barrier = pltpu.get_barrier_semaphore()
    peers = [p_dev, q_dev, c_dev] + x_devs + y_devs
    for dev in peers:
        pl.semaphore_signal(barrier, inc=1, device_id=dev, device_id_type=MESH)
    pl.semaphore_wait(barrier, len(peers))

    def rows(c):
        return pl.ds(pl.multiple_of(c * CH, CH), CH)

    def half(c):
        return pl.ds(pl.multiple_of(lax.rem(c, 2) * CH, CH), CH)

    def small(c):
        return pl.ds(pl.multiple_of(c * SM, SM), SM)

    def part(c):
        return pl.ds(pl.multiple_of(lax.rem(c, 4) * SM, SM), SM)

    def span(c, n):
        return pl.ds(pl.multiple_of(c * n, SM), n)

    def inside(c, n):
        return pl.ds(pl.multiple_of(lax.rem(c, BLK // n) * n, SM), n)

    def f_copy(c):
        return remote(f_hbm.at[small(c)], fp.at[small(c)], f_send.at[c], f_recv.at[c], p_dev)

    def t_copy(c):
        return remote(t_hbm.at[small(c)], tq.at[c // 4, part(c)], t_send.at[c], t_recv.at[c], q_dev)

    def di_copy(c):
        return remote(si.at[small(c)], ri.at[small(c)], di_send.at[c], di_recv.at[c], p_dev)

    def dt_copy(c):
        return remote(st.at[small(c)], rt.at[small(c)], dt_send.at[c], dt_recv.at[c], q_dev)

    for c in range(NSM):
        f_copy(c).start()
        t_copy(c).start()
    w_in = pltpu.make_async_copy(w_hbm, w, in_sem.at[0])
    f_in = pltpu.make_async_copy(f_hbm, fn, in_sem.at[1])
    t_in = pltpu.make_async_copy(t_hbm, tn, in_sem.at[2])
    w_in.start()
    f_in.start()
    t_in.start()

    for copy in scalars:
        copy.wait()
    scale = scale_ref[0]
    offset = offset_ref[0]

    def pair(g, h):
        first = cap_ref[g, 0, 0, h]
        a0, a1, live = img_ref[g, 0, 0, h], img_ref[g, 0, 1, h], cnt_ref[g, 0, h]
        out = []
        for k in range(2):
            slot = jnp.abs(first - k)
            out.append((a0 + (a1 - a0) * slot, jnp.clip(live - slot, 0, 1).astype(F32)))
        return out

    pair_a, pair_b, pair_c = pair(gp, me), pair(me, gq), pair(gp, gq)

    def hit(sel, b):
        return (1 - jnp.abs(sel - b)).astype(F32)

    def norm(v):
        return lax.rsqrt(jnp.sum(v * v, axis=-1, keepdims=True) + EPS)

    def project(g, u, r):
        return (g - u * jnp.sum(g * u, axis=-1, keepdims=True)) * r

    def loop(n, body, start=0):
        lax.fori_loop(start, n, lambda i, _: (body(i), 0)[1], 0)

    def embed(f_ref, where):
        e = mm(f_ref[where, :], w[...], NN)
        r = norm(e)
        return e * r, r

    w_in.wait()
    f_in.wait()

    def embed_own(c):
        unit, r = embed(fn, rows(c))
        unit32[rows(c), :] = unit
        inv[rows(c), 0:1] = r
        iun[c // 2, half(c), :] = unit.astype(BF)

    loop(NCH, embed_own)
    t_in.wait()

    def text_own(c):
        v = tn[rows(c), :].astype(F32)
        r = norm(v)
        inv[rows(c), 2:3] = r
        tun[c // 2, half(c), :] = (v * r).astype(BF)

    loop(NCH, text_own)

    def line(b, start, n):
        return pl.ds(pl.multiple_of(b * BLK + start, SM), n)

    def tile(images, sel, texts, k, slot, live, diagonal):
        def body(r):
            s = mm(images[sel, half(r), :], texts[k], NT) * scale + offset
            if diagonal:
                on = (lax.broadcasted_iota(jnp.int32, s.shape, 0) + r * CH) == lax.broadcasted_iota(jnp.int32, s.shape, 1)
                s = jnp.where(on, -s, s)
            e = jnp.exp(s)
            g = e / (1.0 + e)
            if diagonal:
                g = jnp.where(on, -g, g)
            else:
                g = g * live
            gs[slot, half(r), :] = g.astype(BF)
            total = jnp.sum(jnp.log1p(e), axis=1, keepdims=True)
            return total

        return body

    def tile_diag(k):
        body = tile(iun, k, tun, k, k, None, True)

        def step(r):
            inv[line(k, r * CH, CH), 3:4] = body(r)

        loop(2, step)

    def tile_own(k, slot):
        sel, live = pair_b[k]
        body = tile(iun, sel, tq, k, slot, live, False)

        def step(r):
            total = body(r) * live
            for b in range(2):
                where = line(b, r * CH, CH)
                inv[where, 3:4] = inv[where, 3:4] + total * hit(sel, b)

        loop(2, step)

    def piece(b, r0, nr, k, c0, nc):
        sel, live = pair_c[k]
        keep = live * hit(sel, b)
        e = jnp.exp(mm(iup[b, r0 : r0 + nr, :], tq[k, c0 : c0 + nc, :], NT) * scale + offset)
        gs[8 + 2 * k + b, r0 : r0 + nr, c0 : c0 + nc] = (e / (1.0 + e) * keep).astype(BF)
        where = pl.ds(b * BLK + r0, nr)
        inv[where, 4:5] = inv[where, 4:5] + jnp.sum(jnp.log1p(e), axis=1, keepdims=True) * keep

    loop(2, tile_diag)

    def own_diag(c):
        b = c // 2
        din[rows(c), :] = mm(gs[b, half(c), :], tun[b], NN) * scale

    loop(NCH, own_diag)

    def arrive_image(c):
        f_copy(c).wait_recv()
        unit, r = embed(fp, small(c))
        wide[small(c), :] = unit
        inv[small(c), 1:2] = r
        inv[small(c), 4:5] = jnp.zeros((SM, 1), F32)
        iup[c // 4, part(c), :] = unit.astype(BF)

    def near(c):
        b = c // 4
        total = inv[small(c), 4:5]
        for k in range(2):
            sel, live = pair_a[k]
            keep = live * hit(sel, b)
            e = jnp.exp(mm(iup[b, part(c), :], tun[k], NT) * scale + offset)
            gs[2 + 2 * k + b, part(c), :] = (e / (1.0 + e) * keep).astype(BF)
            total = total + jnp.sum(jnp.log1p(e), axis=1, keepdims=True) * keep
        inv[small(c), 4:5] = total

    def arrive_text(c):
        t_copy(c).wait_recv()
        v = tq[c // 4, part(c), :].astype(F32)
        tq[c // 4, part(c), :] = (v * norm(v)).astype(BF)

    def arrive(c):
        arrive_image(c)
        near(c)
        arrive_text(c)

    loop(4, arrive)
    tile_own(0, 6)

    def back_text(cols, parts):
        out = None
        for slot, images, sel in parts:
            v = mm(gs[slot, :, cols], images[sel], TN)
            out = v if out is None else out + v
        return out * scale

    def back_image(b, lines, parts):
        out = None
        for slot, texts, k, sel in parts:
            g = gs[slot, lines, :]
            if sel is not None:
                g = (g.astype(F32) * hit(sel, b)).astype(BF)
            v = mm(g, texts[k], NN)
            out = v if out is None else out + v
        return out * scale

    def own_first(c):
        din[rows(c), :] = din[rows(c), :] + back_image(c // 2, half(c), ((6, tq, 0, pair_b[0][0]),))

    loop(NCH, own_first)
    piece(0, 0, 256, 0, 0, 512)
    piece(0, 256, 256, 0, 0, 512)
    loop(6, arrive, 4)
    piece(1, 0, 256, 0, 0, 512)
    piece(1, 0, 256, 1, 0, 256)
    piece(0, 0, 512, 1, 0, 256)
    loop(7, arrive, 6)
    piece(1, 256, 128, 0, 0, 512)
    piece(1, 256, 128, 1, 0, 384)
    piece(0, 0, 512, 1, 256, 128)
    piece(1, 0, 256, 1, 256, 128)
    def send_text(c, n=CH):
        k = c // (BLK // n)
        sel_b = jnp.where(k == 0, pair_b[0][0], pair_b[1][0])
        sel_c = jnp.where(k == 0, pair_c[0][0], pair_c[1][0])
        v = back_text(inside(c, n), ((6 + k, iun, sel_b), (8 + 2 * k + sel_c, iup, sel_c)))
        st[span(c, n), :] = v.astype(BF)
        for i in range(n // SM):
            dt_copy(c * (n // SM) + i).start()

    def send_image(c, n=CH, held=0):
        b = c // (BLK // n)
        g = back_image(
            b, inside(c, n), ((2 + b, tun, 0, None), (4 + b, tun, 1, None), (8 + b, tq, 0, None), (10 + b, tq, 1, None))
        )
        si[span(c, n), :] = g.astype(BF)
        for i in range(n // SM - held):
            di_copy(c * (n // SM) + i).start()
        ep[span(c, n), :] = project(g, wide[span(c, n), :], inv[span(c, n), 1:2]).astype(BF)

    start = back_image(0, pl.ds(0, SM), ((2, tun, 0, None), (4, tun, 1, None), (8, tq, 0, None)))
    pre[0] = start + mm(gs[10, 0:SM, 0:384], tq[1, 0:384, :], NN) * scale
    pre[1] = back_text(pl.ds(0, SM), ((6, iun, pair_b[0][0]),))
    loop(NSM, arrive_text, NSM - 1)
    piece(0, 0, 512, 1, 384, 128)
    first_image = pre[0] + mm(gs[10, 0:SM, 384:512], tq[1, 384:512, :], NN) * scale
    si[0:SM, :] = first_image.astype(BF)
    loop(1, lambda c: di_copy(c).start())
    pre[0] = first_image
    loop(NSM, arrive_image, NSM - 1)
    piece(1, 384, 128, 0, 0, 512)
    first_text = pre[1] + back_text(pl.ds(0, SM), ((8 + pair_c[0][0], iup, pair_c[0][0]),))
    st[0:SM, :] = first_text.astype(BF)
    loop(1, lambda c: dt_copy(c).start())
    ep[0:SM, :] = project(pre[0], wide[0:SM, :], inv[0:SM, 1:2]).astype(BF)
    loop(2, lambda c: send_image(c, SM), 1)
    loop(2, lambda c: send_text(c, SM), 1)
    loop(NSM, near, NSM - 1)
    piece(1, 384, 128, 1, 0, 512)
    piece(1, 0, 384, 1, 384, 128)
    loop(NCH - 1, send_image, 1)
    loop(NCH, lambda c: send_image(c, CH, 1), NCH - 1)
    loop(2, send_text, 1)

    def row_form(at_col, out):
        for i in range(8):
            v = inv[pl.ds(i * 128, 128), at_col : at_col + 1]
            out[pl.ds(i, 1), :] = jnp.transpose(jnp.broadcast_to(v, (128, 128)))[0:1, :]

    row_form(4, ls)
    l_copy = remote(ls, lr, l_sem.at[0], l_sem.at[1], p_dev)
    l_copy.start()
    tile_own(1, 7)

    def own_image(c):
        g = din[rows(c), :] + back_image(c // 2, half(c), ((7, tq, 1, pair_b[1][0]),))
        din[rows(c), :] = g
        tun[c // 2, half(c), :] = project(g, unit32[rows(c), :], inv[rows(c), 0:1]).astype(BF)

    loop(NCH, own_image)

    def head(cols, hs, by_y):
        def step(j):
            own = pl.ds(pl.multiple_of(j * 384, 128), 384)
            h = mm(fp[:, own], ep[:, cols], TN)
            h = h + mm(fn[pl.ds(0, BLK), own], tun[0, :, cols], TN) + mm(fn[pl.ds(BLK, BLK), own], tun[1, :, cols], TN)
            wide[own, cols] = h

        loop(3, step)

        def split(j):
            v = []
            for i in range(4):
                at_row = (j * 4 + i if by_y else i * 4 + j) * 2 * HR
                v.append(wide[pl.ds(pl.multiple_of(at_row, 8), 2 * HR), cols])
            for c in range(2):
                hs[c, j] = jnp.concatenate([u[c * HR : (c + 1) * HR, :] for u in v], axis=0).astype(BF)

        loop(4, split)

    lo_cols, hi_cols = pl.ds(0, LO), pl.ds(LO, HI)
    head(lo_cols, hs_lo, False)
    c_lo = remote(hs_lo.at[1 - core], rc_lo, c_sem.at[0], c_sem.at[1], c_dev)
    c_lo.start()
    head(hi_cols, hs_hi, True)
    c_hi = remote(hs_hi.at[1 - core], rc_hi, c_sem.at[2], c_sem.at[3], c_dev)
    c_hi.start()

    def add_core(rc, hs):
        def step(j):
            rc[j] = (rc[j].astype(F32) + hs[core, j].astype(F32)).astype(BF)

        loop(4, step)

    c_lo.wait()
    add_core(rc_lo, hs_lo)
    xc = [remote(rc_lo.at[xs[d]], rx.at[d], x_send.at[d], x_recv.at[d], x_devs[d]) for d in range(3)]
    for copy in xc:
        copy.start()
    loop(NCH, send_text, 2)
    c_hi.wait()
    add_core(rc_hi, hs_hi)
    yc = [
        remote(rc_hi.at[ys[d]], ry.at[d], y_send.at[d], y_recv.at[d], y_devs[d]) for d in range(3)
    ]
    for copy in yc:
        copy.start()

    def own_text(c):
        b = c // 2
        sel = jnp.where(b == 0, pair_a[0][0], pair_a[1][0])
        v = mm(gs[b, :, half(c)], iun[b], TN) + mm(gs[2 + 2 * b + sel, :, half(c)], iup[sel], TN)
        wide[rows(c), :] = v * scale

    loop(NCH, own_text)

    def finish(c, n=CH):
        where = span(c, n)
        b = c // (BLK // n)
        for i in range(n // SM):
            dt_copy(c * (n // SM) + i).wait_recv()
        u = tn[where, :].astype(F32) * inv[where, 2:3]
        gt = wide[where, :] + rt[where, :].astype(F32)
        iun[b, inside(c, n), :] = project(gt, u, inv[where, 2:3]).astype(BF)
        for i in range(n // SM):
            di_copy(c * (n // SM) + i).wait_recv()
        g = din[where, :] + ri[where, :].astype(F32)
        eg = project(g, unit32[where, :], inv[where, 0:1]).astype(BF)
        iup[b, inside(c, n), :] = mm(eg, w[...], NT).astype(BF)

    loop(2, finish)

    def fold(rc, mine, recv, out):
        v = rc[mine].astype(F32)
        for d in range(3):
            v = v + recv[d].astype(F32)
        zero = jnp.zeros((HP - HR, v.shape[1]), F32)
        for i in range(4):
            out[i] = jnp.concatenate([v[i * HR : (i + 1) * HR, :], zero], axis=0).astype(BF)

    for copy in xc:
        copy.wait()
    fold(rc_lo, x, rx, ba)
    second = [remote(ba.at[ys[d]], r2a.at[d], y2_send.at[d], y2_recv.at[d], y_devs[d]) for d in range(3)]
    for copy in second:
        copy.start()
    def sent(c):
        f_copy(c).wait_send()
        t_copy(c).wait_send()

    loop(NSM, sent)
    for copy in yc:
        copy.wait()
    fold(rc_hi, y, ry, bb)
    third = [remote(bb.at[xs[d]], r2b.at[d], x2_send.at[d], x2_recv.at[d], x_devs[d]) for d in range(3)]
    for copy in third:
        copy.start()
    loop(3, finish, 2)
    for copy in second + third:
        copy.wait()
    lo = ba[y].astype(F32)
    hi = bb[x].astype(F32)
    for d in range(3):
        lo = lo + r2a[d].astype(F32)
        hi = hi + r2b[d].astype(F32)
    v = jnp.concatenate([lo, hi], axis=1)
    last = [v[32:HR, i * 384 : (i + 1) * 384] for i in range(3)] + [jnp.zeros((4, 384), F32)]
    zs[0] = v[0:32, :].astype(BF)
    zt[0] = jnp.concatenate(last, axis=0).astype(BF)

    def z_copies(step, dev):
        pairs = ((zs, zr), (zt, zu))
        return [
            remote(a.at[step], b.at[step], z_send.at[2 * step + i], z_recv.at[2 * step + i], dev)
            for i, (a, b) in enumerate(pairs)
        ]

    z0 = z_copies(0, p_dev)
    for copy in z0:
        copy.start()
    di_copy(NSM - 1).start()
    for copy in z0:
        copy.wait()
    zs[1] = (zs[0].astype(F32) + zr[0].astype(F32)).astype(BF)
    zt[1] = (zt[0].astype(F32) + zu[0].astype(F32)).astype(BF)
    z1 = z_copies(1, q_dev)
    for copy in z1:
        copy.start()
    def returned(c):
        di_copy(c).wait_send()
        dt_copy(c).wait_send()

    loop(NSM - 2, returned)
    l_copy.wait()
    row_form(3, ls)
    loss_out[...] = (ls[...] + lr[...]) * (1.0 / BLK)
    loop(NSM - 1, lambda c: finish(c, SM), NSM - 2)
    loop(NSM, lambda c: finish(c, SM), NSM - 1)
    for copy in z1:
        copy.wait()
    head_out[0:32, :] = zs[1].astype(F32) + zr[1].astype(F32)
    last = zt[1].astype(F32) + zu[1].astype(F32)
    for i in range(3):
        head_out[32:HR, i * 384 : (i + 1) * 384] = last[4 * i : 4 * i + 4, :]

    loop(NSM, returned, NSM - 2)


def emit(loss, pooled, text, grad, loss_out, pooled_out, text_out, grad_out, line, sem):
    copies = [pltpu.make_async_copy(grad, grad_out, sem.at[8])]
    for i in range(4):
        where = pl.ds(i % 2 * CH, CH)
        copies.append(pltpu.make_async_copy(pooled.at[i // 2, where], pooled_out.at[i // 2, where], sem.at[i]))
        copies.append(pltpu.make_async_copy(text.at[i // 2, where], text_out.at[i // 2, where], sem.at[4 + i]))
    for copy in copies:
        copy.start()
    for i in range(8):
        line[pl.ds(i * 128, 128)] = loss[i, :]
    copies.append(pltpu.make_async_copy(line, loss_out, sem.at[9]))
    copies[-1].start()
    for copy in copies:
        copy.wait()


def per_device(features, captions, head, scaling, offset, img, cap, cnt):
    hbm = pl.BlockSpec(memory_space=pl.ANY)
    smem = pl.BlockSpec(memory_space=pltpu.SMEM)
    vmem = pl.BlockSpec(memory_space=pltpu.VMEM)
    big = pltpu.VMEM((ROWS, D), BF)
    blocks = pltpu.VMEM((2, BLK, D), BF)
    dma = pltpu.SemaphoreType.DMA
    loss, pooled, text, grad = pl.pallas_call(
        kernel,
        out_shape=(pltpu.VMEM((8, 128), F32), blocks, blocks, pltpu.VMEM((HR, D), F32)),
        in_specs=[hbm] * 3 + [smem] * 2 + [hbm] * 3,
        out_specs=(vmem, vmem, vmem, vmem),
        scratch_shapes=[
            pltpu.SMEM((4, 1, 2, 4), jnp.int32), pltpu.SMEM((4, 1, 2, 4), jnp.int32), pltpu.SMEM((4, 1, 4), jnp.int32),
            big, big, big, blocks, blocks, pltpu.VMEM((D, D), BF),
            pltpu.VMEM((ROWS, D), F32), pltpu.VMEM((ROWS, D), F32), pltpu.VMEM((D, D), F32),
            big, big, big, big, pltpu.VMEM((12, BLK, BLK), BF), big,
            pltpu.VMEM((2, 4, 4 * HR, LO), BF), pltpu.VMEM((2, 4, 4 * HR, HI), BF),
            pltpu.VMEM((4, 4 * HR, LO), BF), pltpu.VMEM((4, 4 * HR, HI), BF),
            pltpu.VMEM((3, 4 * HR, LO), BF), pltpu.VMEM((3, 4 * HR, HI), BF),
            pltpu.VMEM((4, HP, LO), BF), pltpu.VMEM((4, HP, HI), BF),
            pltpu.VMEM((3, HP, LO), BF), pltpu.VMEM((3, HP, HI), BF),
            pltpu.VMEM((2, 32, D), BF), pltpu.VMEM((2, 32, D), BF), pltpu.VMEM((2, 16, 384), BF), pltpu.VMEM((2, 16, 384), BF),
            pltpu.VMEM((2, SM, D), F32),
            pltpu.VMEM((ROWS, 5), F32),
            pltpu.VMEM((8, 128), F32), pltpu.VMEM((8, 128), F32),
            dma((NSM,)), dma((NSM,)), dma((NSM,)), dma((NSM,)), dma((NSM,)), dma((NSM,)), dma((NSM,)), dma((NSM,)),
            dma((2,)), dma((4,)), dma((3,)), dma((3,)), dma((3,)), dma((3,)), dma((3,)), dma((3,)), dma((3,)), dma((3,)),
            dma((4,)), dma((4,)), dma((6,)),
        ],
        compiler_params=pltpu.CompilerParams(
            collective_id=0, has_side_effects=True, vmem_limit_bytes=57 << 20
        ),
        cost_estimate=pl.CostEstimate(flops=34_000_000_000, bytes_accessed=20_000_000, transcendentals=6_000_000),
    )(features, captions, head, scaling, offset, jnp.swapaxes(img, 2, 3), jnp.swapaxes(cap, 2, 3), cnt)
    loss, pooled, text, grad = pl.pallas_call(
        emit,
        out_shape=(
            jax.ShapeDtypeStruct((ROWS,), F32),
            jax.ShapeDtypeStruct((2, BLK, D), BF),
            jax.ShapeDtypeStruct((2, BLK, D), BF),
            jax.ShapeDtypeStruct((HR, D), F32),
        ),
        in_specs=[vmem, hbm, hbm, hbm],
        out_specs=(hbm, hbm, hbm, hbm),
        scratch_shapes=[pltpu.VMEM((ROWS,), F32), dma((10,))],
        compiler_params=pltpu.CompilerParams(vmem_limit_bytes=4 << 20),
    )(*(pltpu.with_memory_space_constraint(v, pltpu.VMEM) for v in (loss, pooled, text, grad)))
    return loss, pooled.reshape(ROWS, D), text.reshape(ROWS, D), grad


def solution(mesh):
    return jax.shard_map(
        per_device,
        mesh=mesh,
        in_specs=(
            P(("grp", "inner"), None),
            P(("grp", "inner"), None),
            P(),
            P(),
            P(),
            P(None, "inner", None, None),
            P(None, "inner", None, None),
            P(None, "inner", None),
        ),
        out_specs=(
            P(("grp", "inner")),
            P(("grp", "inner"), None),
            P(("grp", "inner"), None),
            P("inner", None),
        ),
        check_vma=False,
    )
```

```python
import functools

import jax
import jax.numpy as jnp
from jax import lax
from jax.experimental import pallas as pl
from jax.experimental.pallas import tpu as pltpu
from jax.sharding import PartitionSpec as P

MESH = pl.DeviceIdType.MESH
BLK = 512
D = 1152
ROWS = 1024
CH = 256
NCH = ROWS // CH
SM = 128
NSM = ROWS // SM
EPS = 1e-06
HR = 36
HP = 48
LO = 640
HI = D - LO
BF = jnp.bfloat16
F32 = jnp.float32

NN = (((1,), (0,)), ((), ()))
NT = (((1,), (1,)), ((), ()))
TN = (((0,), (0,)), ((), ()))


def mm(a, b, dims):
    return lax.dot_general(a, b, dims, preferred_element_type=F32)


def kernel(
    f_hbm, t_hbm, w_hbm, scale_ref, offset_ref, img_hbm, cap_hbm, cnt_hbm,
    loss_out, iup, iun, head_out,
    img_ref, cap_ref, cnt_ref,
    fn, fp, tn, tun, tq, w, unit32, din, wide, si, st, ri, rt, gs, ep,
    hs_lo, hs_hi, rc_lo, rc_hi, rx, ry, ba, bb, r2a, r2b, zs, zr, zt, zu, pre, inv, ls, lr,
    f_send, f_recv, t_send, t_recv, di_send, di_recv, dt_send, dt_recv,
    l_sem, c_sem, x_send, x_recv, y_send, y_recv, x2_send, x2_recv, y2_send, y2_recv,
    z_send, z_recv, in_sem,
):
    me = lax.axis_index("grp")
    inner = lax.axis_index("inner")
    odd = lax.rem(me, 2)
    gp = lax.rem(me + 3 + 2 * odd, 4)
    gq = lax.rem(me + 1 + 2 * odd, 4)
    core = lax.rem(inner, 2)
    x = lax.rem(inner // 2, 4)
    y = inner // 8

    def at(yy, xx, cc):
        return (yy * 4 + xx) * 2 + cc

    p_dev, q_dev = (gp, inner), (gq, inner)
    c_dev = (me, at(y, x, 1 - core))
    xs = [lax.rem(x + d, 4) for d in (1, 2, 3)]
    ys = [lax.rem(y + d, 4) for d in (1, 2, 3)]
    x_devs = [(me, at(y, v, core)) for v in xs]
    y_devs = [(me, at(v, x, core)) for v in ys]

    def remote(src, dst, send, recv, dev):
        return pltpu.make_async_remote_copy(
            src_ref=src, dst_ref=dst, send_sem=send, recv_sem=recv, device_id=dev, device_id_type=MESH
        )

    scalars = [
        pltpu.make_async_copy(src, dst, in_sem.at[3 + i])
        for i, (src, dst) in enumerate(((img_hbm, img_ref), (cap_hbm, cap_ref), (cnt_hbm, cnt_ref)))
    ]
    for copy in scalars:
        copy.start()
    barrier = pltpu.get_barrier_semaphore()
    peers = [p_dev, q_dev, c_dev] + x_devs + y_devs
    for dev in peers:
        pl.semaphore_signal(barrier, inc=1, device_id=dev, device_id_type=MESH)
    pl.semaphore_wait(barrier, len(peers))

    def rows(c):
        return pl.ds(pl.multiple_of(c * CH, CH), CH)

    def half(c):
        return pl.ds(pl.multiple_of(lax.rem(c, 2) * CH, CH), CH)

    def small(c):
        return pl.ds(pl.multiple_of(c * SM, SM), SM)

    def part(c):
        return pl.ds(pl.multiple_of(lax.rem(c, 4) * SM, SM), SM)

    def span(c, n):
        return pl.ds(pl.multiple_of(c * n, SM), n)

    def inside(c, n):
        return pl.ds(pl.multiple_of(lax.rem(c, BLK // n) * n, SM), n)

    def f_copy(c):
        return remote(f_hbm.at[small(c)], fp.at[small(c)], f_send.at[c], f_recv.at[c], p_dev)

    def t_copy(c):
        return remote(t_hbm.at[small(c)], tq.at[c // 4, part(c)], t_send.at[c], t_recv.at[c], q_dev)

    def di_copy(c):
        return remote(si.at[small(c)], ri.at[small(c)], di_send.at[c], di_recv.at[c], p_dev)

    def dt_copy(c):
        return remote(st.at[small(c)], rt.at[small(c)], dt_send.at[c], dt_recv.at[c], q_dev)

    for c in range(NSM):
        f_copy(c).start()
        t_copy(c).start()
    w_in = pltpu.make_async_copy(w_hbm, w, in_sem.at[0])
    f_in = pltpu.make_async_copy(f_hbm, fn, in_sem.at[1])
    t_in = pltpu.make_async_copy(t_hbm, tn, in_sem.at[2])
    w_in.start()
    f_in.start()
    t_in.start()

    for copy in scalars:
        copy.wait()
    scale = scale_ref[0]
    offset = offset_ref[0]

    def pair(g, h):
        first = cap_ref[g, 0, 0, h]
        a0, a1, live = img_ref[g, 0, 0, h], img_ref[g, 0, 1, h], cnt_ref[g, 0, h]
        out = []
        for k in range(2):
            slot = jnp.abs(first - k)
            out.append((a0 + (a1 - a0) * slot, jnp.clip(live - slot, 0, 1).astype(F32)))
        return out

    pair_a, pair_b, pair_c = pair(gp, me), pair(me, gq), pair(gp, gq)

    def hit(sel, b):
        return (1 - jnp.abs(sel - b)).astype(F32)

    def norm(v):
        return lax.rsqrt(jnp.sum(v * v, axis=-1, keepdims=True) + EPS)

    def project(g, u, r):
        return (g - u * jnp.sum(g * u, axis=-1, keepdims=True)) * r

    def loop(n, body, start=0):
        lax.fori_loop(start, n, lambda i, _: (body(i), 0)[1], 0)

    def embed(f_ref, where):
        e = mm(f_ref[where, :], w[...], NN)
        r = norm(e)
        return e * r, r

    w_in.wait()
    f_in.wait()

    def embed_own(c):
        unit, r = embed(fn, rows(c))
        unit32[rows(c), :] = unit
        inv[rows(c), 0:1] = r
        iun[c // 2, half(c), :] = unit.astype(BF)

    loop(NCH, embed_own)
    t_in.wait()

    def text_own(c):
        v = tn[rows(c), :].astype(F32)
        r = norm(v)
        inv[rows(c), 2:3] = r
        tun[c // 2, half(c), :] = (v * r).astype(BF)

    loop(NCH, text_own)

    def line(b, start, n):
        return pl.ds(pl.multiple_of(b * BLK + start, SM), n)

    def tile(images, sel, texts, k, slot, live, diagonal):
        def body(r):
            s = mm(images[sel, half(r), :], texts[k], NT) * scale + offset
            if diagonal:
                on = (lax.broadcasted_iota(jnp.int32, s.shape, 0) + r * CH) == lax.broadcasted_iota(jnp.int32, s.shape, 1)
                s = jnp.where(on, -s, s)
            e = jnp.exp(s)
            g = e / (1.0 + e)
            if diagonal:
                g = jnp.where(on, -g, g)
            else:
                g = g * live
            gs[slot, half(r), :] = g.astype(BF)
            total = jnp.sum(jnp.log1p(e), axis=1, keepdims=True)
            return total

        return body

    def tile_diag(k):
        body = tile(iun, k, tun, k, k, None, True)

        def step(r):
            inv[line(k, r * CH, CH), 3:4] = body(r)

        loop(2, step)

    def tile_own(k, slot):
        sel, live = pair_b[k]
        body = tile(iun, sel, tq, k, slot, live, False)

        def step(r):
            total = body(r) * live
            for b in range(2):
                where = line(b, r * CH, CH)
                inv[where, 3:4] = inv[where, 3:4] + total * hit(sel, b)

        loop(2, step)

    def piece(b, r0, nr, k, c0, nc):
        sel, live = pair_c[k]
        keep = live * hit(sel, b)
        e = jnp.exp(mm(iup[b, r0 : r0 + nr, :], tq[k, c0 : c0 + nc, :], NT) * scale + offset)
        gs[8 + 2 * k + b, r0 : r0 + nr, c0 : c0 + nc] = (e / (1.0 + e) * keep).astype(BF)
        where = pl.ds(b * BLK + r0, nr)
        inv[where, 4:5] = inv[where, 4:5] + jnp.sum(jnp.log1p(e), axis=1, keepdims=True) * keep

    loop(2, tile_diag)

    def own_diag(c):
        b = c // 2
        din[rows(c), :] = mm(gs[b, half(c), :], tun[b], NN) * scale

    loop(NCH, own_diag)

    def arrive_image(c):
        f_copy(c).wait_recv()
        unit, r = embed(fp, small(c))
        wide[small(c), :] = unit
        inv[small(c), 1:2] = r
        inv[small(c), 4:5] = jnp.zeros((SM, 1), F32)
        iup[c // 4, part(c), :] = unit.astype(BF)

    def near(c):
        b = c // 4
        total = inv[small(c), 4:5]
        for k in range(2):
            sel, live = pair_a[k]
            keep = live * hit(sel, b)
            e = jnp.exp(mm(iup[b, part(c), :], tun[k], NT) * scale + offset)
            gs[2 + 2 * k + b, part(c), :] = (e / (1.0 + e) * keep).astype(BF)
            total = total + jnp.sum(jnp.log1p(e), axis=1, keepdims=True) * keep
        inv[small(c), 4:5] = total

    def arrive_text(c):
        t_copy(c).wait_recv()
        v = tq[c // 4, part(c), :].astype(F32)
        tq[c // 4, part(c), :] = (v * norm(v)).astype(BF)

    def arrive(c):
        arrive_image(c)
        near(c)
        arrive_text(c)

    loop(4, arrive)
    tile_own(0, 6)

    def back_text(cols, parts):
        out = None
        for slot, images, sel in parts:
            v = mm(gs[slot, :, cols], images[sel], TN)
            out = v if out is None else out + v
        return out * scale

    def back_image(b, lines, parts):
        out = None
        for slot, texts, k, sel in parts:
            g = gs[slot, lines, :]
            if sel is not None:
                g = (g.astype(F32) * hit(sel, b)).astype(BF)
            v = mm(g, texts[k], NN)
            out = v if out is None else out + v
        return out * scale

    def own_first(c):
        din[rows(c), :] = din[rows(c), :] + back_image(c // 2, half(c), ((6, tq, 0, pair_b[0][0]),))

    loop(NCH, own_first)
    piece(0, 0, 256, 0, 0, 512)
    piece(0, 256, 256, 0, 0, 512)
    loop(6, arrive, 4)
    piece(1, 0, 256, 0, 0, 512)
    piece(1, 0, 256, 1, 0, 256)
    piece(0, 0, 512, 1, 0, 256)
    loop(7, arrive, 6)
    piece(1, 256, 128, 0, 0, 512)
    piece(1, 256, 128, 1, 0, 384)
    piece(0, 0, 512, 1, 256, 128)
    piece(1, 0, 256, 1, 256, 128)
    def send_text(c, n=CH):
        k = c // (BLK // n)
        sel_b = jnp.where(k == 0, pair_b[0][0], pair_b[1][0])
        sel_c = jnp.where(k == 0, pair_c[0][0], pair_c[1][0])
        v = back_text(inside(c, n), ((6 + k, iun, sel_b), (8 + 2 * k + sel_c, iup, sel_c)))
        st[span(c, n), :] = v.astype(BF)
        for i in range(n // SM):
            dt_copy(c * (n // SM) + i).start()

    def send_image(c, n=CH, held=0):
        b = c // (BLK // n)
        g = back_image(
            b, inside(c, n), ((2 + b, tun, 0, None), (4 + b, tun, 1, None), (8 + b, tq, 0, None), (10 + b, tq, 1, None))
        )
        si[span(c, n), :] = g.astype(BF)
        for i in range(n // SM - held):
            di_copy(c * (n // SM) + i).start()
        ep[span(c, n), :] = project(g, wide[span(c, n), :], inv[span(c, n), 1:2]).astype(BF)

    start = back_image(0, pl.ds(0, SM), ((2, tun, 0, None), (4, tun, 1, None), (8, tq, 0, None)))
    pre[0] = start + mm(gs[10, 0:SM, 0:384], tq[1, 0:384, :], NN) * scale
    pre[1] = back_text(pl.ds(0, SM), ((6, iun, pair_b[0][0]),))
    loop(NSM, arrive_text, NSM - 1)
    piece(0, 0, 512, 1, 384, 128)
    first_image = pre[0] + mm(gs[10, 0:SM, 384:512], tq[1, 384:512, :], NN) * scale
    si[0:SM, :] = first_image.astype(BF)
    loop(1, lambda c: di_copy(c).start())
    pre[0] = first_image
    loop(NSM, arrive_image, NSM - 1)
    piece(1, 384, 128, 0, 0, 512)
    first_text = pre[1] + back_text(pl.ds(0, SM), ((8 + pair_c[0][0], iup, pair_c[0][0]),))
    st[0:SM, :] = first_text.astype(BF)
    loop(1, lambda c: dt_copy(c).start())
    ep[0:SM, :] = project(pre[0], wide[0:SM, :], inv[0:SM, 1:2]).astype(BF)
    loop(2, lambda c: send_image(c, SM), 1)
    loop(2, lambda c: send_text(c, SM), 1)
    loop(NSM, near, NSM - 1)
    piece(1, 384, 128, 1, 0, 512)
    piece(1, 0, 384, 1, 384, 128)
    loop(NCH - 1, send_image, 1)
    loop(NCH, lambda c: send_image(c, CH, 1), NCH - 1)
    loop(2, send_text, 1)

    def row_form(at_col, out):
        for i in range(8):
            v = inv[pl.ds(i * 128, 128), at_col : at_col + 1]
            out[pl.ds(i, 1), :] = jnp.transpose(jnp.broadcast_to(v, (128, 128)))[0:1, :]

    row_form(4, ls)
    l_copy = remote(ls, lr, l_sem.at[0], l_sem.at[1], p_dev)
    l_copy.start()
    tile_own(1, 7)

    def own_image(c):
        g = din[rows(c), :] + back_image(c // 2, half(c), ((7, tq, 1, pair_b[1][0]),))
        din[rows(c), :] = g
        tun[c // 2, half(c), :] = project(g, unit32[rows(c), :], inv[rows(c), 0:1]).astype(BF)

    loop(NCH, own_image)

    def head(cols, hs, by_y):
        def step(j):
            own = pl.ds(pl.multiple_of(j * 384, 128), 384)
            h = mm(fp[:, own], ep[:, cols], TN)
            h = h + mm(fn[pl.ds(0, BLK), own], tun[0, :, cols], TN) + mm(fn[pl.ds(BLK, BLK), own], tun[1, :, cols], TN)
            wide[own, cols] = h

        loop(3, step)

        def split(j):
            v = []
            for i in range(4):
                at_row = (j * 4 + i if by_y else i * 4 + j) * 2 * HR
                v.append(wide[pl.ds(pl.multiple_of(at_row, 8), 2 * HR), cols])
            for c in range(2):
                hs[c, j] = jnp.concatenate([u[c * HR : (c + 1) * HR, :] for u in v], axis=0).astype(BF)

        loop(4, split)

    lo_cols, hi_cols = pl.ds(0, LO), pl.ds(LO, HI)
    head(lo_cols, hs_lo, False)
    c_lo = remote(hs_lo.at[1 - core], rc_lo, c_sem.at[0], c_sem.at[1], c_dev)
    c_lo.start()
    head(hi_cols, hs_hi, True)
    c_hi = remote(hs_hi.at[1 - core], rc_hi, c_sem.at[2], c_sem.at[3], c_dev)
    c_hi.start()

    def add_core(rc, hs):
        def step(j):
            rc[j] = (rc[j].astype(F32) + hs[core, j].astype(F32)).astype(BF)

        loop(4, step)

    c_lo.wait()
    add_core(rc_lo, hs_lo)
    xc = [remote(rc_lo.at[xs[d]], rx.at[d], x_send.at[d], x_recv.at[d], x_devs[d]) for d in range(3)]
    for copy in xc:
        copy.start()
    loop(NCH, send_text, 2)
    c_hi.wait()
    add_core(rc_hi, hs_hi)
    yc = [
        remote(rc_hi.at[ys[d]], ry.at[d], y_send.at[d], y_recv.at[d], y_devs[d]) for d in range(3)
    ]
    for copy in yc:
        copy.start()

    def own_text(c):
        b = c // 2
        sel = jnp.where(b == 0, pair_a[0][0], pair_a[1][0])
        v = mm(gs[b, :, half(c)], iun[b], TN) + mm(gs[2 + 2 * b + sel, :, half(c)], iup[sel], TN)
        wide[rows(c), :] = v * scale

    loop(NCH, own_text)

    def finish(c, n=CH):
        where = span(c, n)
        b = c // (BLK // n)
        for i in range(n // SM):
            dt_copy(c * (n // SM) + i).wait_recv()
        u = tn[where, :].astype(F32) * inv[where, 2:3]
        gt = wide[where, :] + rt[where, :].astype(F32)
        iun[b, inside(c, n), :] = project(gt, u, inv[where, 2:3]).astype(BF)
        for i in range(n // SM):
            di_copy(c * (n // SM) + i).wait_recv()
        g = din[where, :] + ri[where, :].astype(F32)
        eg = project(g, unit32[where, :], inv[where, 0:1]).astype(BF)
        iup[b, inside(c, n), :] = mm(eg, w[...], NT).astype(BF)

    loop(2, finish)

    def fold(rc, mine, recv, out):
        v = rc[mine].astype(F32)
        for d in range(3):
            v = v + recv[d].astype(F32)
        zero = jnp.zeros((HP - HR, v.shape[1]), F32)
        for i in range(4):
            out[i] = jnp.concatenate([v[i * HR : (i + 1) * HR, :], zero], axis=0).astype(BF)

    for copy in xc:
        copy.wait()
    fold(rc_lo, x, rx, ba)
    second = [remote(ba.at[ys[d]], r2a.at[d], y2_send.at[d], y2_recv.at[d], y_devs[d]) for d in range(3)]
    for copy in second:
        copy.start()

    def sent(c):
        f_copy(c).wait_send()
        t_copy(c).wait_send()

    loop(NSM, sent)
    for copy in yc:
        copy.wait()
    fold(rc_hi, y, ry, bb)
    third = [remote(bb.at[xs[d]], r2b.at[d], x2_send.at[d], x2_recv.at[d], x_devs[d]) for d in range(3)]
    for copy in third:
        copy.start()
    for copy in second + third:
        copy.wait()
    lo = ba[y].astype(F32)
    hi = bb[x].astype(F32)
    for d in range(3):
        lo = lo + r2a[d].astype(F32)
        hi = hi + r2b[d].astype(F32)
    v = jnp.concatenate([lo, hi], axis=1)
    last = [v[32:HR, i * 384 : (i + 1) * 384] for i in range(3)] + [jnp.zeros((4, 384), F32)]
    zs[0] = v[0:32, :].astype(BF)
    zt[0] = jnp.concatenate(last, axis=0).astype(BF)

    def z_copies(step, dev):
        pairs = ((zs, zr), (zt, zu))
        return [
            remote(a.at[step], b.at[step], z_send.at[2 * step + i], z_recv.at[2 * step + i], dev)
            for i, (a, b) in enumerate(pairs)
        ]

    z0 = z_copies(0, p_dev)
    for copy in z0:
        copy.start()
    di_copy(NSM - 1).start()
    loop(3, finish, 2)
    for copy in z0:
        copy.wait()
    zs[1] = (zs[0].astype(F32) + zr[0].astype(F32)).astype(BF)
    zt[1] = (zt[0].astype(F32) + zu[0].astype(F32)).astype(BF)
    z1 = z_copies(1, q_dev)
    for copy in z1:
        copy.start()
    def returned(c):
        di_copy(c).wait_send()
        dt_copy(c).wait_send()

    loop(NSM - 2, returned)
    l_copy.wait()
    row_form(3, ls)
    loss_out[...] = (ls[...] + lr[...]) * (1.0 / BLK)
    loop(NSM - 1, lambda c: finish(c, SM), NSM - 2)
    loop(NSM, lambda c: finish(c, SM), NSM - 1)
    for copy in z1:
        copy.wait()
    head_out[0:32, :] = zs[1].astype(F32) + zr[1].astype(F32)
    last = zt[1].astype(F32) + zu[1].astype(F32)
    for i in range(3):
        head_out[32:HR, i * 384 : (i + 1) * 384] = last[4 * i : 4 * i + 4, :]

    loop(NSM, returned, NSM - 2)


def emit(loss, pooled, text, grad, loss_out, pooled_out, text_out, grad_out, line, sem):
    copies = [pltpu.make_async_copy(grad, grad_out, sem.at[8])]
    for i in range(4):
        where = pl.ds(i % 2 * CH, CH)
        copies.append(pltpu.make_async_copy(pooled.at[i // 2, where], pooled_out.at[i // 2, where], sem.at[i]))
        copies.append(pltpu.make_async_copy(text.at[i // 2, where], text_out.at[i // 2, where], sem.at[4 + i]))
    for copy in copies:
        copy.start()
    for i in range(8):
        line[pl.ds(i * 128, 128)] = loss[i, :]
    copies.append(pltpu.make_async_copy(line, loss_out, sem.at[9]))
    copies[-1].start()
    for copy in copies:
        copy.wait()


def per_device(features, captions, head, scaling, offset, img, cap, cnt):
    hbm = pl.BlockSpec(memory_space=pl.ANY)
    smem = pl.BlockSpec(memory_space=pltpu.SMEM)
    vmem = pl.BlockSpec(memory_space=pltpu.VMEM)
    big = pltpu.VMEM((ROWS, D), BF)
    blocks = pltpu.VMEM((2, BLK, D), BF)
    dma = pltpu.SemaphoreType.DMA
    loss, pooled, text, grad = pl.pallas_call(
        kernel,
        out_shape=(pltpu.VMEM((8, 128), F32), blocks, blocks, pltpu.VMEM((HR, D), F32)),
        in_specs=[hbm] * 3 + [smem] * 2 + [hbm] * 3,
        out_specs=(vmem, vmem, vmem, vmem),
        scratch_shapes=[
            pltpu.SMEM((4, 1, 2, 4), jnp.int32), pltpu.SMEM((4, 1, 2, 4), jnp.int32), pltpu.SMEM((4, 1, 4), jnp.int32),
            big, big, big, blocks, blocks, pltpu.VMEM((D, D), BF),
            pltpu.VMEM((ROWS, D), F32), pltpu.VMEM((ROWS, D), F32), pltpu.VMEM((D, D), F32),
            big, big, big, big, pltpu.VMEM((12, BLK, BLK), BF), big,
            pltpu.VMEM((2, 4, 4 * HR, LO), BF), pltpu.VMEM((2, 4, 4 * HR, HI), BF),
            pltpu.VMEM((4, 4 * HR, LO), BF), pltpu.VMEM((4, 4 * HR, HI), BF),
            pltpu.VMEM((3, 4 * HR, LO), BF), pltpu.VMEM((3, 4 * HR, HI), BF),
            pltpu.VMEM((4, HP, LO), BF), pltpu.VMEM((4, HP, HI), BF),
            pltpu.VMEM((3, HP, LO), BF), pltpu.VMEM((3, HP, HI), BF),
            pltpu.VMEM((2, 32, D), BF), pltpu.VMEM((2, 32, D), BF), pltpu.VMEM((2, 16, 384), BF), pltpu.VMEM((2, 16, 384), BF),
            pltpu.VMEM((2, SM, D), F32),
            pltpu.VMEM((ROWS, 5), F32),
            pltpu.VMEM((8, 128), F32), pltpu.VMEM((8, 128), F32),
            dma((NSM,)), dma((NSM,)), dma((NSM,)), dma((NSM,)), dma((NSM,)), dma((NSM,)), dma((NSM,)), dma((NSM,)),
            dma((2,)), dma((4,)), dma((3,)), dma((3,)), dma((3,)), dma((3,)), dma((3,)), dma((3,)), dma((3,)), dma((3,)),
            dma((4,)), dma((4,)), dma((6,)),
        ],
        compiler_params=pltpu.CompilerParams(
            collective_id=0, has_side_effects=True, vmem_limit_bytes=57 << 20
        ),
        cost_estimate=pl.CostEstimate(flops=34_000_000_000, bytes_accessed=20_000_000, transcendentals=6_000_000),
    )(features, captions, head, scaling, offset, jnp.swapaxes(img, 2, 3), jnp.swapaxes(cap, 2, 3), cnt)
    loss, pooled, text, grad = pl.pallas_call(
        emit,
        out_shape=(
            jax.ShapeDtypeStruct((ROWS,), F32),
            jax.ShapeDtypeStruct((2, BLK, D), BF),
            jax.ShapeDtypeStruct((2, BLK, D), BF),
            jax.ShapeDtypeStruct((HR, D), F32),
        ),
        in_specs=[vmem, hbm, hbm, hbm],
        out_specs=(hbm, hbm, hbm, hbm),
        scratch_shapes=[pltpu.VMEM((ROWS,), F32), dma((10,))],
        compiler_params=pltpu.CompilerParams(vmem_limit_bytes=4 << 20),
    )(*(pltpu.with_memory_space_constraint(v, pltpu.VMEM) for v in (loss, pooled, text, grad)))
    return loss, pooled.reshape(ROWS, D), text.reshape(ROWS, D), grad


def solution(mesh):
    return jax.shard_map(
        per_device,
        mesh=mesh,
        in_specs=(
            P(("grp", "inner"), None),
            P(("grp", "inner"), None),
            P(),
            P(),
            P(),
            P(None, "inner", None, None),
            P(None, "inner", None, None),
            P(None, "inner", None),
        ),
        out_specs=(
            P(("grp", "inner")),
            P(("grp", "inner"), None),
            P(("grp", "inner"), None),
            P("inner", None),
        ),
        check_vma=False,
    )
```
